512 devices in a mesh: dp: 32 (over y, x, core), mp: 16 (over z).
Axes of the slice: x: 4, y: 4, z: 16, core: 2. Of those that a mesh axis runs over, the one named last changes fastest.
Arguments:
- tokens: bfloat16 [4096, 8192], P('dp', 'mp'), may hold values from -6 to 6
- cotangent: bfloat16 [4096, 8192], P('dp', 'mp'), may hold values from -6 to 6
- up_weight: bfloat16 [5, 256, 32768], P(None, 'dp', 'mp'), may hold values from -0.15625 to 0.15625
- down_weight: bfloat16 [5, 256, 32768], P(None, 'dp', 'mp'), may hold values from -0.078125 to 0.078125
Outputs:
- mixed: bfloat16 [4096, 8192], P('dp', 'mp')
- grad_tokens: bfloat16 [4096, 8192], P('dp', 'mp')
The draws below stay inside these ranges and needn't reach their ends.
All inputs are finite; a program needn't handle non-finite values.
Results may differ from the reference program's by a relative error of at most 0.0049.
Values may be sent and summed in bfloat16 or wider, within the bound.
A program may use at most 64 MiB of HBM per device.

```python
import jax
import jax.numpy as jnp
from jax import lax

D = 8192
FF = 32768
BLK = 256
LEVELS = 4
TOK_DEV = 128
TERMS = 5
HB = 1024
TOKENS = 4096


def level_of(own_key, dims, shards, least, largest):
    gain, own = 1.0, jax.random.fold_in(own_key, 6)
    for position, blocks in shards:
        draws = jnp.exp(jax.random.uniform(jax.random.fold_in(own, position), (blocks,), jnp.float32, least / len(shards), largest / len(shards)))
        gain = gain * jnp.repeat(draws, dims[position] // blocks).reshape([-1 if axis == position else 1 for axis in range(len(dims))])
    return gain


def bell_draw(stream_key, shape, scale, most, pieces=(), held_as=jnp.bfloat16):
    gain = level_of(stream_key, shape, pieces, -0.22, 0.18) if pieces else 1.0
    drawn = jax.random.normal(stream_key, shape, jnp.float32) * scale * gain
    return jnp.minimum(jnp.maximum(drawn, -most), most).astype(held_as)


def setup_inputs(seed: int = 0) -> dict:
    key_list = jax.random.split(jax.random.key(seed), 5)
    return {
        "tokens": bell_draw(key_list[0], (TOKENS, D), 1.0, 6.0, ((0, 32), (1, 16))),
        "cotangent": bell_draw(key_list[1], (TOKENS, D), 1.0, 6.0, ((0, 32), (1, 16))),
        "up_weight": bell_draw(key_list[2], (TERMS, BLK, FF), (TERMS * BLK) ** -0.5, 0.15625, ((1, 32), (2, 16))),
        "down_weight": bell_draw(key_list[3], (TERMS, BLK, FF), (TERMS * HB) ** -0.5, 0.078125, ((1, 32), (2, 16))),
    }


def shuffle_blocks(blocks, block_shift):
    order = jnp.bitwise_xor(jnp.arange(blocks.shape[1], dtype=jnp.int32), jnp.int32(block_shift))
    return jnp.take(blocks, order, axis=1)

def one_group(token_rows, cot_rows, up_terms, down_terms, shifts):
    block_count = D // BLK
    tok_count = token_rows.shape[0]
    token_blocks = token_rows.reshape(tok_count, block_count, BLK).astype(jnp.float32)
    cot_blocks = cot_rows.reshape(tok_count, block_count, BLK).astype(jnp.float32)
    pre_act = jnp.zeros((tok_count, block_count, FF // block_count), jnp.float32)
    for term_idx in range(TERMS):
        moved = shuffle_blocks(token_blocks, shifts[term_idx])
        pre_act = pre_act + jnp.einsum('tbi,ibh->tbh', moved, up_terms[term_idx])
    hidden = jax.nn.gelu(pre_act).astype(jnp.bfloat16).astype(jnp.float32)
    mixed = jnp.zeros((tok_count, block_count, BLK), jnp.float32)
    grad_hidden = jnp.zeros_like(pre_act)
    for term_idx in range(TERMS):
        part_out = jnp.einsum('tbh,jbh->tbj', hidden, down_terms[term_idx])
        mixed = mixed + shuffle_blocks(part_out, shifts[term_idx])
        moved = shuffle_blocks(cot_blocks, shifts[term_idx])
        grad_hidden = grad_hidden + jnp.einsum('tbj,jbh->tbh', moved, down_terms[term_idx])
    grad_pre = jax.vjp(jax.nn.gelu, pre_act)[1](grad_hidden)[0]
    grad_pre = grad_pre.astype(jnp.bfloat16).astype(jnp.float32)
    grad_tokens = jnp.zeros((tok_count, block_count, BLK), jnp.float32)
    for term_idx in range(TERMS):
        part_grad = jnp.einsum('tbh,ibh->tbi', grad_pre, up_terms[term_idx])
        grad_tokens = grad_tokens + shuffle_blocks(part_grad, shifts[term_idx])
    return (mixed.reshape(tok_count, D).astype(jnp.bfloat16), grad_tokens.reshape(tok_count, D).astype(jnp.bfloat16))

def reference(tokens, cotangent, up_weight, down_weight):
    block_count = D // BLK
    hidden_per = FF // block_count
    up_terms = up_weight.astype(jnp.float32).reshape(TERMS, BLK, block_count, hidden_per)
    down_terms = down_weight.astype(jnp.float32).reshape(TERMS, BLK, block_count, hidden_per)
    shifts = [0] + [1 << level_idx + 1 for level_idx in range(LEVELS)]
    groups = tokens.shape[0] // TOK_DEV
    token_groups = tokens.reshape(groups, TOK_DEV, D)
    cot_groups = cotangent.reshape(groups, TOK_DEV, D)

    def run_group(pair):
        return one_group(pair[0], pair[1], up_terms, down_terms, shifts)
    mixed, grad_tokens = lax.map(run_group, (token_groups, cot_groups))
    return (mixed.reshape(tokens.shape[0], D), grad_tokens.reshape(tokens.shape[0], D))
```

```python
import math

import jax
import jax.numpy as jnp
from jax import lax
from jax.experimental import pallas as pl
from jax.experimental.pallas import tpu as pltpu
from jax.sharding import PartitionSpec as P

BLK = 256
TERMS = 5
HB = 1024
TOK = 128
SIDE = 4
MESH = pl.DeviceIdType.MESH
ROOT = math.sqrt(2.0 / math.pi)
CUBE = 0.044715

Q4, Q2, Q1A, Q1B, Q0A, Q0B, Q0C = range(7)


def xor_step(bit, amount):
    return amount - 2 * amount * bit


class Sends:
    def __init__(self, send_sem, recv_sem):
        self.send_sem, self.recv_sem = send_sem, recv_sem
        self.sent, self.received, self.open = 0, 0, []

    def slot(self):
        self.received += 1
        return self.received - 1

    def copy(self, src, dst, slot, device):
        copy = pltpu.make_async_remote_copy(
            src_ref=src, dst_ref=dst, send_sem=self.send_sem.at[self.sent],
            recv_sem=self.recv_sem.at[slot], device_id=device, device_id_type=MESH,
        )
        self.sent += 1
        return copy

    def start(self, src, dst, slot, device, when=None):
        copy = self.copy(src, dst, slot, device)
        self.open.append((copy, when))
        if when is None:
            copy.start()
        else:
            pl.when(when)(copy.start)

    def arrive(self, dst, slot, device):
        pltpu.make_async_remote_copy(
            src_ref=dst, dst_ref=dst, send_sem=self.send_sem.at[0],
            recv_sem=self.recv_sem.at[slot], device_id=device, device_id_type=MESH,
        ).wait_recv()

    def drain(self):
        for copy, when in self.open:
            if when is None:
                copy.wait_send()
            else:
                pl.when(when)(copy.wait_send)
        self.open = []


def kernel(tok, cot, up, down, out_mixed, out_grad,
           x_all, c_all, wu, wd, stage, terms, sendbuf, landed, hidden, slope, gpre,
           local_sem, send_sem, recv_sem):
    dp = lax.axis_index("dp")
    z = lax.axis_index("mp")
    core = lax.rem(dp, 2)
    chip = lax.div(dp, 2)
    px, py = lax.rem(chip, SIDE), lax.div(chip, SIDE)
    a = px * (1 - core) + py * core
    b = py * (1 - core) + px * core

    def chip_at(a_pos, b_pos):
        return a_pos * (1 + 3 * core) + b_pos * (4 - 3 * core)

    def ring(pos, step):
        return lax.rem(pos + step + SIDE, SIDE)

    def plane(a_pos, b_pos):
        return (chip_at(a_pos, b_pos) * 2 + core, z)

    b0 = lax.rem(z, 2)
    b1 = lax.rem(lax.div(z, 2), 2)
    b2 = lax.rem(lax.div(z, 4), 2)
    b3 = lax.rem(lax.div(z, 8), 2)
    d1, d2, d4, d8 = xor_step(b0, 1), xor_step(b1, 2), xor_step(b2, 4), xor_step(b3, 8)
    c01 = b0 != b1
    c12 = b1 != b2
    c02 = b0 != b2
    n01 = b0 == b1
    far = jnp.logical_and(c12, c02)
    mid4 = jnp.logical_and(b1 == b2, c02)
    own4 = jnp.logical_and(b1 == b2, b0 == b2)

    def along(step):
        return (dp, z + step)

    sibling = (dp + 1 - 2 * core, z)
    sends = Sends(send_sem, recv_sem)

    mine = pl.ds(pl.multiple_of(core * BLK, BLK), BLK)
    theirs = pl.ds(pl.multiple_of((1 - core) * BLK, BLK), BLK)
    own_rows = pl.ds(pl.multiple_of(core * TOK, TOK), TOK)
    sib_rows = pl.ds(pl.multiple_of((1 - core) * TOK, TOK), TOK)
    own_units = pl.ds(pl.multiple_of(core * HB, HB), HB)
    sib_units = pl.ds(pl.multiple_of((1 - core) * HB, HB), HB)
    acts, alls = (tok, cot), (x_all, c_all)
    weights, gathered = (up, down), (wu, wd)

    local = []
    for n in range(2):
        local.append(pltpu.make_async_copy(acts[n].at[:, mine], alls[n].at[0, own_rows, :], local_sem.at[n]))
        local.append(pltpu.make_async_copy(weights[n].at[:, :, own_units], stage.at[n, 0], local_sem.at[2 + n]))
    for copy in local:
        copy.start()

    barrier = pltpu.get_barrier_semaphore()
    a_up, a_down, b_up, b_down = (
        plane(ring(a, 1), b), plane(ring(a, -1), b), plane(a, ring(b, 1)), plane(a, ring(b, -1)))
    greet = [sibling, a_up, a_down, b_up, b_down]
    greet += [along(s) for s in (d1, d2, d4, d1 + d2, d1 + d4, d2 + d4, d4 + d8)]
    for device in greet:
        pl.semaphore_signal(barrier, inc=1, device_id=device, device_id_type=MESH)
    pl.semaphore_wait(barrier, len(greet))

    swap_act = [sends.slot() for _ in range(2)]
    swap_w = [sends.slot() for _ in range(2)]
    for n in range(2):
        sends.start(acts[n].at[:, theirs], alls[n].at[0, own_rows, :], swap_act[n], sibling)
        sends.start(weights[n].at[:, :, sib_units], stage.at[n, 1], swap_w[n], sibling)

    act_slot = [[[sends.slot() for _ in range(5)] for _ in range(2)] for _ in range(2)]
    act_rows = (own_rows, sib_rows)

    def act_send(n, ch, src, dst, device, when=None):
        rows = act_rows[ch]
        sends.start(alls[n].at[src, rows, :], alls[n].at[dst, rows, :], act_slot[n][ch][dst], device, when)

    def act_wait(n, ch, dst):
        sends.arrive(alls[n].at[dst, act_rows[ch], :], act_slot[n][ch][dst], sibling)

    def act_own(n, ch):
        if ch == 0:
            local[2 * n].wait()
        else:
            sends.arrive(alls[n].at[0, sib_rows, :], swap_act[n], sibling)
        act_send(n, ch, 0, 1, along(d1))
        act_send(n, ch, 0, 2, along(d2), c01)
        act_send(n, ch, 0, 3, along(d4), far)

    def act_one(n, ch):
        act_wait(n, ch, 1)
        act_send(n, ch, 1, 2, along(d1 + d2), c01)
        act_send(n, ch, 1, 3, along(d1 + d4), far)

    def act_two(n, ch):
        act_wait(n, ch, 2)
        act_send(n, ch, 2, 3, along(d2 + d4), c12)

    def act_four(n, ch):
        act_wait(n, ch, 3)
        act_send(n, ch, 3, 4, along(d4 + d8))

    def act_end(n, ch):
        act_wait(n, ch, 4)

    w_slot = [[sends.slot() for _ in range(20)] for _ in range(2)]
    ks = (a, ring(a, -1), ring(a, 1), ring(a, 2))
    lo, hi, whole = pl.ds(0, HB // 2), pl.ds(HB // 2, HB // 2), pl.ds(0, HB)

    def piece(n, a_pos, b_pos, cols):
        rows = pl.ds(pl.multiple_of(chip_at(a_pos, b_pos) * 16, 16), 16)
        return gathered[n].at[:, rows, cols]

    def w_send(n, a_pos, b_pos, cols, slot, device):
        ref = piece(n, a_pos, b_pos, cols)
        sends.start(ref, ref, w_slot[n][slot], device)

    def w_wait(n, a_pos, b_pos, cols, slot):
        sends.arrive(piece(n, a_pos, b_pos, cols), w_slot[n][slot], sibling)

    def w_across(n, k):
        w_send(n, ks[k], b, whole, 4 + k, b_up)
        w_send(n, ks[k], b, whole, 8 + k, b_down)

    def w_start(n):
        local[2 * n + 1].wait()
        sends.arrive(stage.at[n, 1], swap_w[n], sibling)
        first = stage[n, 0].astype(jnp.float32)
        second = stage[n, 1].astype(jnp.float32)
        rows = pl.ds(pl.multiple_of(chip * 16, 16), 16)

        @pl.when(core == 0)
        def _():
            gathered[n][:, rows, :] = jnp.concatenate([first, second], axis=1).astype(jnp.bfloat16)

        @pl.when(core == 1)
        def _():
            gathered[n][:, rows, :] = jnp.concatenate([second, first], axis=1).astype(jnp.bfloat16)

        w_send(n, a, b, whole, 0, a_up)
        w_send(n, a, b, whole, 1, a_down)
        w_across(n, 0)

    def w_near(n):
        w_wait(n, ks[1], b, whole, 0)
        w_send(n, ks[1], b, lo, 2, a_up)
        w_wait(n, ks[2], b, whole, 1)
        w_send(n, ks[2], b, hi, 3, a_down)
        w_across(n, 1)
        w_across(n, 2)

    def w_far(n):
        w_wait(n, ks[3], b, lo, 2)
        w_wait(n, ks[3], b, hi, 3)
        w_across(n, 3)

    def w_pass(n, k):
        w_wait(n, ks[k], ring(b, -1), whole, 4 + k)
        w_send(n, ks[k], ring(b, -1), lo, 12 + k, b_up)
        w_wait(n, ks[k], ring(b, 1), whole, 8 + k)
        w_send(n, ks[k], ring(b, 1), hi, 16 + k, b_down)

    def w_end(n):
        for k in range(4):
            w_wait(n, ks[k], ring(b, 2), lo, 12 + k)
            w_wait(n, ks[k], ring(b, 2), hi, 16 + k)

    TILE = 256

    def product(all_ref, w_ref, cols):
        total = None
        for s in range(TERMS):
            part = jnp.dot(all_ref[s], w_ref[s, :, cols], preferred_element_type=jnp.float32)
            total = part if total is None else total + part
        return total

    def forward():
        def body(tile, carry):
            cols = pl.ds(pl.multiple_of(tile * TILE, TILE), TILE)
            pre = product(x_all, wu, cols)
            th = jnp.tanh(ROOT * (pre + CUBE * pre * pre * pre))
            hidden[:, cols] = (0.5 * pre * (1.0 + th)).astype(jnp.bfloat16)
            inner = ROOT * (1.0 + 3.0 * CUBE * pre * pre)
            slope[:, cols] = 0.5 * (1.0 + th) + 0.5 * pre * (1.0 - th * th) * inner
            return carry
        lax.fori_loop(0, HB // TILE, body, 0)

    def backward():
        def body(tile, carry):
            cols = pl.ds(pl.multiple_of(tile * TILE, TILE), TILE)
            gpre[:, cols] = (product(c_all, wd, cols) * slope[:, cols]).astype(jnp.bfloat16)
            return carry
        lax.fori_loop(0, HB // TILE, body, 0)

    def term(o, s):
        act_ref, w_ref = ((hidden, wd), (gpre, wu))[o]
        terms[o, s] = lax.dot_general(
            act_ref[...], w_ref[s], (((1,), (1,)), ((), ())), preferred_element_type=jnp.float32)

    sum_slot = [[[sends.slot() for _ in range(7)] for _ in range(2)] for _ in range(2)]
    out_slot = [sends.slot() for _ in range(2)]
    sum_rows = (sib_rows, own_rows)
    outs = (out_mixed, out_grad)
    last = []

    def sum_send(o, ch, s, place, device, when=None):
        rows = sum_rows[ch]
        sends.start(sendbuf.at[o, s, rows, :], landed.at[o, place, rows, :], sum_slot[o][ch][place], device, when)

    def sum_add(o, ch, s, place, when=None):
        rows = sum_rows[ch]

        def add():
            sends.arrive(landed.at[o, place, rows, :], sum_slot[o][ch][place], sibling)
            terms[o, s, rows, :] += landed[o, place, rows, :].astype(jnp.float32)
        if when is None:
            add()
        else:
            pl.when(when)(add)

    def sum_round(o, ch, s):
        rows = sum_rows[ch]
        sendbuf[o, s, rows, :] = terms[o, s, rows, :].astype(jnp.bfloat16)

    def sum_eight(o, ch):
        sum_round(o, ch, 4)
        sum_send(o, ch, 4, Q4, along(d4 + d8))

    def sum_four(o, ch):
        sum_add(o, ch, 3, Q4)
        sum_round(o, ch, 3)
        sum_send(o, ch, 3, Q2, along(d2 + d4), c12)
        sum_send(o, ch, 3, Q1B, along(d1 + d4), mid4)
        sum_send(o, ch, 3, Q0C, along(d4), own4)

    def sum_two(o, ch):
        sum_add(o, ch, 2, Q2, c12)
        sum_round(o, ch, 2)
        sum_send(o, ch, 2, Q1A, along(d1 + d2), c01)
        sum_send(o, ch, 2, Q0B, along(d2), n01)

    def sum_one(o, ch):
        sum_add(o, ch, 1, Q1A, c01)
        sum_add(o, ch, 1, Q1B, far)
        sum_round(o, ch, 1)
        sum_send(o, ch, 1, Q0A, along(d1))

    def sum_own(o, ch):
        sum_add(o, ch, 0, Q0A)
        sum_add(o, ch, 0, Q0B, c01)
        sum_add(o, ch, 0, Q0C, far)
        sum_round(o, ch, 0)
        if ch == 0:
            sends.start(sendbuf.at[o, 0, sib_rows, :], outs[o].at[:, mine], out_slot[o], sibling)
        else:
            copy = pltpu.make_async_copy(sendbuf.at[o, 0, own_rows, :], outs[o].at[:, mine], local_sem.at[4 + o])
            copy.start()
            last.append(copy)

    T, C = 0, 1
    act_own(T, 0)
    w_start(0)
    act_own(T, 1)
    act_one(T, 0)
    w_near(0)
    act_own(C, 0)
    act_one(T, 1)
    act_two(T, 0)
    w_far(0)
    w_pass(0, 0)
    w_start(1)
    act_own(C, 1)
    act_one(C, 0)
    act_two(T, 1)
    act_four(T, 0)
    w_pass(0, 1)
    w_near(1)
    act_one(C, 1)
    act_two(C, 0)
    act_four(T, 1)
    w_pass(0, 2)
    w_pass(0, 3)
    w_far(1)
    act_two(C, 1)
    act_four(C, 0)
    w_end(0)
    w_pass(1, 0)
    w_pass(1, 1)
    act_end(T, 0)
    act_end(T, 1)
    act_four(C, 1)
    forward()
    w_pass(1, 2)
    w_pass(1, 3)
    w_end(1)
    for s in (4, 3):
        term(0, s)
        if s == 4:
            sum_eight(0, 0)
            sum_eight(0, 1)
    act_end(C, 0)
    act_end(C, 1)
    backward()
    term(1, 4)
    sum_eight(1, 0)
    sum_eight(1, 1)
    term(0, 2)
    sum_four(0, 0)
    term(0, 1)
    sum_four(0, 1)
    term(0, 0)
    sum_two(0, 0)
    term(1, 3)
    sum_two(0, 1)
    sum_four(1, 0)
    term(1, 2)
    sum_one(0, 0)
    sum_four(1, 1)
    term(1, 1)
    sum_one(0, 1)
    sum_two(1, 0)
    term(1, 0)
    sum_own(0, 0)
    sum_two(1, 1)
    sum_one(1, 0)
    sum_own(0, 1)
    sum_one(1, 1)
    sum_own(1, 0)
    sum_own(1, 1)
    for o in range(2):
        sends.arrive(outs[o].at[:, theirs], out_slot[o], sibling)
    for copy in last:
        copy.wait()
    sends.drain()
    assert sends.sent <= 160 and sends.received <= 160


def on_device(tokens, cotangent, up_weight, down_weight):
    any_spec = pl.BlockSpec(memory_space=pl.ANY)
    bf, f32 = jnp.bfloat16, jnp.float32
    return pl.pallas_call(
        kernel,
        out_shape=[jax.ShapeDtypeStruct(tokens.shape, bf)] * 2,
        in_specs=[any_spec] * 4,
        out_specs=[any_spec] * 2,
        scratch_shapes=[
            pltpu.VMEM((TERMS, 2 * TOK, BLK), bf),
            pltpu.VMEM((TERMS, 2 * TOK, BLK), bf),
            pltpu.VMEM((TERMS, BLK, HB), bf),
            pltpu.VMEM((TERMS, BLK, HB), bf),
            pltpu.VMEM((2, 2, TERMS, 8, HB), bf),
            pltpu.VMEM((2, TERMS, 2 * TOK, BLK), f32),
            pltpu.VMEM((2, TERMS, 2 * TOK, BLK), bf),
            pltpu.VMEM((2, 7, 2 * TOK, BLK), bf),
            pltpu.VMEM((2 * TOK, HB), bf),
            pltpu.VMEM((2 * TOK, HB), f32),
            pltpu.VMEM((2 * TOK, HB), bf),
            pltpu.SemaphoreType.DMA((6,)),
            pltpu.SemaphoreType.DMA((160,)),
            pltpu.SemaphoreType.DMA((160,)),
        ],
        compiler_params=pltpu.CompilerParams(
            collective_id=0, has_side_effects=True, vmem_limit_bytes=48 * 1024 * 1024),
    )(tokens, cotangent, up_weight, down_weight)


def solution(mesh):
    act, weight = P("dp", "mp"), P(None, "dp", "mp")
    return jax.shard_map(
        on_device, mesh=mesh, in_specs=(act, act, weight, weight), out_specs=(act, act), check_vma=False)
```

```python
import math

import jax
import jax.numpy as jnp
from jax import lax
from jax.experimental import pallas as pl
from jax.experimental.pallas import tpu as pltpu
from jax.sharding import PartitionSpec as P

BLK = 256
TERMS = 5
HB = 1024
TOK = 128
SIDE = 4
MESH = pl.DeviceIdType.MESH
ROOT = math.sqrt(2.0 / math.pi)
CUBE = 0.044715

Q4, Q0A, Q0B, Q0C = range(4)


def xor_step(bit, amount):
    return amount - 2 * amount * bit


class Sends:
    def __init__(self, send_sem, recv_sem):
        self.send_sem, self.recv_sem = send_sem, recv_sem
        self.sent, self.received, self.open = 0, 0, []

    def slot(self):
        self.received += 1
        return self.received - 1

    def copy(self, src, dst, slot, device):
        copy = pltpu.make_async_remote_copy(
            src_ref=src, dst_ref=dst, send_sem=self.send_sem.at[self.sent],
            recv_sem=self.recv_sem.at[slot], device_id=device, device_id_type=MESH,
        )
        self.sent += 1
        return copy

    def start(self, src, dst, slot, device, when=None):
        copy = self.copy(src, dst, slot, device)
        self.open.append((copy, when))
        if when is None:
            copy.start()
        else:
            pl.when(when)(copy.start)

    def arrive(self, dst, slot, device):
        pltpu.make_async_remote_copy(
            src_ref=dst, dst_ref=dst, send_sem=self.send_sem.at[0],
            recv_sem=self.recv_sem.at[slot], device_id=device, device_id_type=MESH,
        ).wait_recv()

    def drain(self):
        for copy, when in self.open:
            if when is None:
                copy.wait_send()
            else:
                pl.when(when)(copy.wait_send)
        self.open = []


def kernel(tok, cot, up, down, out_mixed, out_grad,
           x_all, c_all, wu, wd, stage, terms, sendbuf, landed, hidden, slope, gpre,
           local_sem, send_sem, recv_sem):
    dp = lax.axis_index("dp")
    z = lax.axis_index("mp")
    core = lax.rem(dp, 2)
    chip = lax.div(dp, 2)
    px, py = lax.rem(chip, SIDE), lax.div(chip, SIDE)
    a = px * (1 - core) + py * core
    b = py * (1 - core) + px * core

    def chip_at(a_pos, b_pos):
        return a_pos * (1 + 3 * core) + b_pos * (4 - 3 * core)

    def ring(pos, step):
        return lax.rem(pos + step + SIDE, SIDE)

    def plane(a_pos, b_pos):
        return (chip_at(a_pos, b_pos) * 2 + core, z)

    b0 = lax.rem(z, 2)
    b1 = lax.rem(lax.div(z, 2), 2)
    b2 = lax.rem(lax.div(z, 4), 2)
    b3 = lax.rem(lax.div(z, 8), 2)
    d1, d2, d4, d8 = xor_step(b0, 1), xor_step(b1, 2), xor_step(b2, 4), xor_step(b3, 8)

    def along(step):
        return (dp, z + step)

    sibling = (dp + 1 - 2 * core, z)
    sends = Sends(send_sem, recv_sem)

    mine = pl.ds(pl.multiple_of(core * BLK, BLK), BLK)
    theirs = pl.ds(pl.multiple_of((1 - core) * BLK, BLK), BLK)
    own_rows = pl.ds(pl.multiple_of(core * TOK, TOK), TOK)
    sib_rows = pl.ds(pl.multiple_of((1 - core) * TOK, TOK), TOK)
    own_units = pl.ds(pl.multiple_of(core * HB, HB), HB)
    sib_units = pl.ds(pl.multiple_of((1 - core) * HB, HB), HB)
    acts, alls = (tok, cot), (x_all, c_all)
    weights, gathered = (up, down), (wu, wd)

    local = []
    for n in range(2):
        local.append(pltpu.make_async_copy(acts[n].at[:, mine], alls[n].at[0, own_rows, :], local_sem.at[n]))
        local.append(pltpu.make_async_copy(weights[n].at[:, :, own_units], stage.at[n, 0], local_sem.at[2 + n]))
    for copy in local:
        copy.start()

    barrier = pltpu.get_barrier_semaphore()
    a_up, a_down, b_up, b_down = (
        plane(ring(a, 1), b), plane(ring(a, -1), b), plane(a, ring(b, 1)), plane(a, ring(b, -1)))
    greet = [sibling, a_up, a_down, b_up, b_down]
    greet += [along(s) for s in (d1, d2, d4, d4 + d8)]
    for device in greet:
        pl.semaphore_signal(barrier, inc=1, device_id=device, device_id_type=MESH)
    pl.semaphore_wait(barrier, len(greet))

    swap_act = [sends.slot() for _ in range(2)]
    swap_w = [sends.slot() for _ in range(2)]
    for n in range(2):
        sends.start(acts[n].at[:, theirs], alls[n].at[0, own_rows, :], swap_act[n], sibling)
        sends.start(weights[n].at[:, :, sib_units], stage.at[n, 1], swap_w[n], sibling)

    act_slot = [[[sends.slot() for _ in range(5)] for _ in range(2)] for _ in range(2)]
    act_rows = (own_rows, sib_rows)

    def act_send(n, ch, src, dst, device, when=None):
        rows = act_rows[ch]
        sends.start(alls[n].at[src, rows, :], alls[n].at[dst, rows, :], act_slot[n][ch][dst], device, when)

    def act_wait(n, ch, dst):
        sends.arrive(alls[n].at[dst, act_rows[ch], :], act_slot[n][ch][dst], sibling)

    def act_four(n, ch):
        act_wait(n, ch, 3)
        act_send(n, ch, 3, 4, along(d4 + d8))

    parts = ((0, 0, 5), (1, 3, 5), (1, 0, 3))
    w_slot = [[sends.slot() for _ in range(20)] for _ in parts]
    ks = (a, ring(a, -1), ring(a, 1), ring(a, 2))
    lo, hi, whole = pl.ds(0, HB // 2), pl.ds(HB // 2, HB // 2), pl.ds(0, HB)

    def piece(n, a_pos, b_pos, cols):
        rows = pl.ds(pl.multiple_of(chip_at(a_pos, b_pos) * 16, 16), 16)
        array, first, end = parts[n]
        return gathered[array].at[first:end, rows, cols]

    def w_send(n, a_pos, b_pos, cols, slot, device):
        ref = piece(n, a_pos, b_pos, cols)
        sends.start(ref, ref, w_slot[n][slot], device)

    def w_wait(n, a_pos, b_pos, cols, slot):
        sends.arrive(piece(n, a_pos, b_pos, cols), w_slot[n][slot], sibling)

    def w_across(n, k):
        w_send(n, ks[k], b, whole, 4 + k, b_up)
        w_send(n, ks[k], b, whole, 8 + k, b_down)

    def w_join(array):
        local[2 * array + 1].wait()
        sends.arrive(stage.at[array, 1], swap_w[array], sibling)
        first = stage[array, 0].astype(jnp.float32)
        second = stage[array, 1].astype(jnp.float32)
        rows = pl.ds(pl.multiple_of(chip * 16, 16), 16)

        @pl.when(core == 0)
        def _():
            gathered[array][:, rows, :] = jnp.concatenate([first, second], axis=1).astype(jnp.bfloat16)

        @pl.when(core == 1)
        def _():
            gathered[array][:, rows, :] = jnp.concatenate([second, first], axis=1).astype(jnp.bfloat16)

    def w_start(n):
        w_send(n, a, b, whole, 0, a_up)
        w_send(n, a, b, whole, 1, a_down)
        w_across(n, 0)

    def w_near(n):
        w_wait(n, ks[1], b, whole, 0)
        w_send(n, ks[1], b, lo, 2, a_up)
        w_wait(n, ks[2], b, whole, 1)
        w_send(n, ks[2], b, hi, 3, a_down)
        w_across(n, 1)
        w_across(n, 2)

    def w_far(n):
        w_wait(n, ks[3], b, lo, 2)
        w_wait(n, ks[3], b, hi, 3)
        w_across(n, 3)

    def w_pass(n, k):
        w_wait(n, ks[k], ring(b, -1), whole, 4 + k)
        w_send(n, ks[k], ring(b, -1), lo, 12 + k, b_up)
        w_wait(n, ks[k], ring(b, 1), whole, 8 + k)
        w_send(n, ks[k], ring(b, 1), hi, 16 + k, b_down)

    def w_end(n):
        for k in range(4):
            w_wait(n, ks[k], ring(b, 2), lo, 12 + k)
            w_wait(n, ks[k], ring(b, 2), hi, 16 + k)

    TILE = 256

    def product(all_ref, w_ref, cols):
        total = None
        for s in range(TERMS):
            part = jnp.dot(all_ref[s], w_ref[s, :, cols], preferred_element_type=jnp.float32)
            total = part if total is None else total + part
        return total

    def forward():
        def body(tile, carry):
            cols = pl.ds(pl.multiple_of(tile * TILE, TILE), TILE)
            pre = product(x_all, wu, cols)
            th = jnp.tanh(ROOT * (pre + CUBE * pre * pre * pre))
            hidden[:, cols] = (0.5 * pre * (1.0 + th)).astype(jnp.bfloat16)
            inner = ROOT * (1.0 + 3.0 * CUBE * pre * pre)
            slope[:, cols] = 0.5 * (1.0 + th) + 0.5 * pre * (1.0 - th * th) * inner
            return carry
        lax.fori_loop(0, HB // TILE, body, 0)

    def backward():
        def body(tile, carry):
            cols = pl.ds(pl.multiple_of(tile * TILE, TILE), TILE)
            gpre[:, cols] = (product(c_all, wd, cols) * slope[:, cols]).astype(jnp.bfloat16)
            return carry
        lax.fori_loop(0, HB // TILE, body, 0)

    def term(o, s):
        act_ref, w_ref = ((hidden, wd), (gpre, wu))[o]
        terms[o, s] = lax.dot_general(
            act_ref[...], w_ref[s], (((1,), (1,)), ((), ())), preferred_element_type=jnp.float32)

    sum_slot = [[[sends.slot() for _ in range(4)] for _ in range(2)] for _ in range(2)]
    out_slot = [sends.slot() for _ in range(2)]
    sum_rows = (sib_rows, own_rows)
    outs = (out_mixed, out_grad)
    last = []

    def sum_send(o, ch, s, place, device, when=None):
        rows = sum_rows[ch]
        sends.start(sendbuf.at[o, s, rows, :], landed.at[o, place, rows, :], sum_slot[o][ch][place], device, when)

    def sum_add(o, ch, s, place, when=None):
        rows = sum_rows[ch]

        def add():
            sends.arrive(landed.at[o, place, rows, :], sum_slot[o][ch][place], sibling)
            terms[o, s, rows, :] += landed[o, place, rows, :].astype(jnp.float32)
        if when is None:
            add()
        else:
            pl.when(when)(add)

    def sum_round(o, ch, s):
        rows = sum_rows[ch]
        sendbuf[o, s, rows, :] = terms[o, s, rows, :].astype(jnp.bfloat16)

    def sum_eight(o, ch):
        sum_round(o, ch, 4)
        sum_send(o, ch, 4, Q4, along(d4 + d8))

    def out_send(o, ch):
        sum_round(o, ch, 0)
        if ch == 0:
            sends.start(sendbuf.at[o, 0, sib_rows, :], outs[o].at[:, mine], out_slot[o], sibling)
        else:
            copy = pltpu.make_async_copy(sendbuf.at[o, 0, own_rows, :], outs[o].at[:, mine], local_sem.at[4 + o])
            copy.start()
            last.append(copy)


    def near_own(n, ch):
        if ch == 0:
            local[2 * n].wait()
        else:
            sends.arrive(alls[n].at[0, sib_rows, :], swap_act[n], sibling)
        act_send(n, ch, 0, 3, along(d4))
        act_send(n, ch, 0, 2, along(d2))
        act_send(n, ch, 0, 1, along(d1))

    def near_end(n, ch):
        act_wait(n, ch, 1)
        act_wait(n, ch, 2)
        act_wait(n, ch, 4)

    def near_two(o, ch):
        sum_round(o, ch, 2)
        sum_send(o, ch, 2, Q0B, along(d2))

    def near_one(o, ch):
        sum_round(o, ch, 1)
        sum_send(o, ch, 1, Q0A, along(d1))

    def near_four(o, ch):
        sum_add(o, ch, 3, Q4)
        sum_round(o, ch, 3)
        sum_send(o, ch, 3, Q0C, along(d4))

    def near_sum(o, ch):
        sum_add(o, ch, 0, Q0A)
        sum_add(o, ch, 0, Q0B)
        sum_add(o, ch, 0, Q0C)
        out_send(o, ch)

    T, C, M, G = 0, 1, 0, 1
    UP, DA, DB = 0, 1, 2
    near_own(T,0)
    w_join(0)
    w_start(UP)
    near_own(T,1)
    w_near(UP)
    w_pass(UP,0)
    act_four(T,0)
    w_far(UP)
    act_four(T,1)
    w_join(1)
    w_start(DA)
    near_own(C,0)
    w_pass(UP,1)
    w_pass(UP,2)
    w_near(DA)
    w_pass(DA,0)
    near_own(C,1)
    w_pass(UP,3)
    w_far(DA)
    w_pass(DA,1)
    w_pass(DA,2)
    w_start(DB)
    w_end(UP)
    w_pass(DA,3)
    w_near(DB)
    w_pass(DB,0)
    act_four(C,0)
    w_far(DB)
    near_end(T,0)
    near_end(T,1)
    forward()
    w_pass(DB,1)
    w_pass(DB,2)
    w_end(DA)
    term(M,4)
    sum_eight(M,0)
    sum_eight(M,1)
    term(M,3)
    act_four(C,1)
    w_pass(DB,3)
    w_end(DB)
    term(M,2)
    near_two(M,0)
    term(M,1)
    near_one(M,0)
    near_four(M,0)
    near_two(M,1)
    near_one(M,1)
    near_four(M,1)
    term(M,0)
    near_end(C,0)
    near_end(C,1)
    backward()
    term(G,4)
    sum_eight(G,0)
    sum_eight(G,1)
    term(G,2)
    near_two(G,0)
    term(G,3)
    near_sum(M,0)
    near_four(G,0)
    near_two(G,1)
    near_four(G,1)
    term(G,1)
    near_one(G,0)
    near_one(G,1)
    near_sum(M,1)
    term(G,0)
    near_sum(G,0)
    near_sum(G,1)
    for o in range(2):
        sends.arrive(outs[o].at[:, theirs], out_slot[o], sibling)
    for copy in last:
        copy.wait()
    sends.drain()
    assert sends.sent <= 160 and sends.received <= 160


def on_device(tokens, cotangent, up_weight, down_weight):
    any_spec = pl.BlockSpec(memory_space=pl.ANY)
    bf, f32 = jnp.bfloat16, jnp.float32
    return pl.pallas_call(
        kernel,
        out_shape=[jax.ShapeDtypeStruct(tokens.shape, bf)] * 2,
        in_specs=[any_spec] * 4,
        out_specs=[any_spec] * 2,
        scratch_shapes=[
            pltpu.VMEM((TERMS, 2 * TOK, BLK), bf),
            pltpu.VMEM((TERMS, 2 * TOK, BLK), bf),
            pltpu.VMEM((TERMS, BLK, HB), bf),
            pltpu.VMEM((TERMS, BLK, HB), bf),
            pltpu.VMEM((2, 2, TERMS, 8, HB), bf),
            pltpu.VMEM((2, TERMS, 2 * TOK, BLK), f32),
            pltpu.VMEM((2, TERMS, 2 * TOK, BLK), bf),
            pltpu.VMEM((2, 4, 2 * TOK, BLK), bf),
            pltpu.VMEM((2 * TOK, HB), bf),
            pltpu.VMEM((2 * TOK, HB), f32),
            pltpu.VMEM((2 * TOK, HB), bf),
            pltpu.SemaphoreType.DMA((6,)),
            pltpu.SemaphoreType.DMA((160,)),
            pltpu.SemaphoreType.DMA((160,)),
        ],
        compiler_params=pltpu.CompilerParams(
            collective_id=0, has_side_effects=True, vmem_limit_bytes=60 * 1024 * 1024),
    )(tokens, cotangent, up_weight, down_weight)


def solution(mesh):
    act, weight = P("dp", "mp"), P(None, "dp", "mp")
    return jax.shard_map(
        on_device, mesh=mesh, in_specs=(act, act, weight, weight), out_specs=(act, act), check_vma=False)
```

```python
import math

import jax
import jax.numpy as jnp
from jax import lax
from jax.experimental import pallas as pl
from jax.experimental.pallas import tpu as pltpu
from jax.sharding import PartitionSpec as P

BLK = 256
TERMS = 5
HB = 1024
TOK = 128
SIDE = 4
MESH = pl.DeviceIdType.MESH
ROOT = math.sqrt(2.0 / math.pi)
CUBE = 0.044715
SEND_SEMS, RECV_SEMS = 13, 58


def xor_step(bit, amount):
    return amount - 2 * amount * bit


class Sends:
    def __init__(self, send_sem, recv_sem):
        self.send_sem, self.recv_sem = send_sem, recv_sem
        self.groups, self.received = 0, 0

    def group(self):
        self.groups += 1
        return self.groups - 1

    def slot(self):
        self.received += 1
        return self.received - 1

    def start(self, src, dst, group, slot, device):
        pltpu.make_async_remote_copy(
            src_ref=src, dst_ref=dst, send_sem=self.send_sem.at[group],
            recv_sem=self.recv_sem.at[slot], device_id=device, device_id_type=MESH,
        ).start()

    def arrive(self, dst, slot, device):
        pltpu.make_async_remote_copy(
            src_ref=dst, dst_ref=dst, send_sem=self.send_sem.at[0],
            recv_sem=self.recv_sem.at[slot], device_id=device, device_id_type=MESH,
        ).wait_recv()

    def left(self, src, group, device):
        pltpu.make_async_remote_copy(
            src_ref=src, dst_ref=src, send_sem=self.send_sem.at[group],
            recv_sem=self.recv_sem.at[0], device_id=device, device_id_type=MESH,
        ).wait_send()


def kernel(tok, cot, up, down, out_mixed, out_grad,
           x_all, c_all, wu, wd, stage, terms, sendbuf, landed, hidden, slope, gpre,
           local_sem, send_sem, recv_sem):
    dp = lax.axis_index("dp")
    z = lax.axis_index("mp")
    core = lax.rem(dp, 2)
    chip = lax.div(dp, 2)
    px, py = lax.rem(chip, SIDE), lax.div(chip, SIDE)
    a = px * (1 - core) + py * core
    b = py * (1 - core) + px * core

    def chip_at(a_pos, b_pos):
        return a_pos * (1 + 3 * core) + b_pos * (4 - 3 * core)

    def ring(pos, step):
        return lax.rem(pos + step + SIDE, SIDE)

    def plane(a_pos, b_pos):
        return (chip_at(a_pos, b_pos) * 2 + core, z)

    b0 = lax.rem(z, 2)
    b1 = lax.rem(lax.div(z, 2), 2)
    b2 = lax.rem(lax.div(z, 4), 2)
    b3 = lax.rem(lax.div(z, 8), 2)
    d1, d2, d4, d8 = xor_step(b0, 1), xor_step(b1, 2), xor_step(b2, 4), xor_step(b3, 8)

    def along(step):
        return (dp, z + step)

    sibling = (dp + 1 - 2 * core, z)
    sends = Sends(send_sem, recv_sem)

    mine = pl.ds(pl.multiple_of(core * BLK, BLK), BLK)
    theirs = pl.ds(pl.multiple_of((1 - core) * BLK, BLK), BLK)
    own_rows = pl.ds(pl.multiple_of(core * TOK, TOK), TOK)
    sib_rows = pl.ds(pl.multiple_of((1 - core) * TOK, TOK), TOK)
    own_units = pl.ds(pl.multiple_of(core * HB, HB), HB)
    sib_units = pl.ds(pl.multiple_of((1 - core) * HB, HB), HB)
    acts, alls = (tok, cot), (x_all, c_all)
    weights, gathered = (up, down), (wu, wd)

    barrier = pltpu.get_barrier_semaphore()
    a_up, a_down, b_up, b_down = (
        plane(ring(a, 1), b), plane(ring(a, -1), b), plane(a, ring(b, 1)), plane(a, ring(b, -1)))
    greet = [along(s) for s in (d4 + d8, d4, d2, d1)]
    greet += [a_up, a_down, b_up, b_down, sibling]
    for device in greet:
        pl.semaphore_signal(barrier, inc=1, device_id=device, device_id_type=MESH)
    local = []
    for n in range(2):
        local.append(pltpu.make_async_copy(acts[n].at[:, mine], alls[n].at[0, own_rows, :], local_sem.at[n]))
        local.append(pltpu.make_async_copy(weights[n].at[:, :, own_units], stage.at[n, 0], local_sem.at[2 + n]))
    for copy in local:
        copy.start()

    pl.semaphore_wait(barrier, len(greet))

    swap_act = [sends.slot() for _ in range(2)]
    swap_w = [sends.slot() for _ in range(2)]
    swap_act_group = [sends.group() for _ in range(2)]
    swap_w_group = [sends.group() for _ in range(2)]
    for n in range(2):
        sends.start(acts[n].at[:, theirs], alls[n].at[0, own_rows, :], swap_act_group[n], swap_act[n], sibling)
        sends.start(weights[n].at[:, :, sib_units], stage.at[n, 1], swap_w_group[n], swap_w[n], sibling)

    near_slot = [[sends.slot() for _ in range(2)] for _ in range(2)]
    four_slot = [[sends.slot() for _ in range(2)] for _ in range(2)]
    act_group = [sends.group() for _ in range(2)]
    act_rows = (own_rows, sib_rows)
    act_place = (0, 1, 2, 4, 3)

    def act_send(n, ch, src, dst, slot, device):
        rows = act_rows[ch]
        sends.start(alls[n].at[src, rows, :], alls[n].at[dst, rows, :], act_group[n], slot[n][ch], device)

    def act_four(n, ch):
        sends.arrive(alls[n].at[4, act_rows[ch], :], four_slot[n][ch], sibling)
        act_send(n, ch, 4, 3, near_slot, along(d4 + d8))

    def near_own(n, ch):
        if ch == 0:
            local[2 * n].wait()
        else:
            sends.arrive(alls[n].at[0, sib_rows, :], swap_act[n], sibling)
        act_send(n, ch, 0, 4, four_slot, along(d4))
        act_send(n, ch, 0, 2, near_slot, along(d2))
        act_send(n, ch, 0, 1, near_slot, along(d1))

    def near_end(n, ch):
        sends.arrive(alls[n].at[1:4, act_rows[ch], :], near_slot[n][ch], sibling)

    parts = ((0, 0, 5), (1, 3, 5), (1, 0, 3))
    w_slot = [[sends.slot() for _ in range(12)] for _ in parts]
    w_group = [sends.group() for _ in parts]
    ks = (a, ring(a, -1), ring(a, 1), ring(a, 2))
    lo, hi, whole = pl.ds(0, HB // 2), pl.ds(HB // 2, HB // 2), pl.ds(0, HB)

    def piece(n, a_pos, b_pos, cols):
        rows = pl.ds(pl.multiple_of(chip_at(a_pos, b_pos) * 16, 16), 16)
        array, first, end = parts[n]
        return gathered[array].at[first:end, rows, cols]

    def w_send(n, a_pos, b_pos, cols, slot, device):
        ref = piece(n, a_pos, b_pos, cols)
        sends.start(ref, ref, w_group[n], w_slot[n][slot], device)

    def w_wait(n, a_pos, b_pos, slot):
        sends.arrive(piece(n, a_pos, b_pos, whole), w_slot[n][slot], sibling)

    def w_across(n, k):
        w_send(n, ks[k], b, whole, 3 + k, b_up)
        w_send(n, ks[k], b, whole, 7 + k, b_down)

    def w_join(array):
        local[2 * array + 1].wait()
        sends.arrive(stage.at[array, 1], swap_w[array], sibling)
        first = stage[array, 0].astype(jnp.float32)
        second = stage[array, 1].astype(jnp.float32)
        rows = pl.ds(pl.multiple_of(chip * 16, 16), 16)

        @pl.when(core == 0)
        def _():
            gathered[array][:, rows, :] = jnp.concatenate([first, second], axis=1).astype(jnp.bfloat16)

        @pl.when(core == 1)
        def _():
            gathered[array][:, rows, :] = jnp.concatenate([second, first], axis=1).astype(jnp.bfloat16)

    def w_start(n):
        w_send(n, a, b, whole, 0, a_up)
        w_send(n, a, b, whole, 1, a_down)
        w_across(n, 0)

    def w_near(n):
        w_wait(n, ks[1], b, 0)
        w_send(n, ks[1], b, lo, 2, a_up)
        w_wait(n, ks[2], b, 1)
        w_send(n, ks[2], b, hi, 2, a_down)
        w_across(n, 1)
        w_across(n, 2)

    def w_far(n):
        w_wait(n, ks[3], b, 2)
        w_across(n, 3)

    def w_pass(n, k):
        w_wait(n, ks[k], ring(b, -1), 3 + k)
        w_send(n, ks[k], ring(b, -1), lo, 11, b_up)
        w_wait(n, ks[k], ring(b, 1), 7 + k)
        w_send(n, ks[k], ring(b, 1), hi, 11, b_down)

    def w_end(n):
        array, first, end = parts[n]
        sends.arrive(gathered[array].at[first:end, 0:64, :], w_slot[n][11], sibling)

    TILE = 256

    def product(all_ref, w_ref, cols):
        total = None
        for s in range(TERMS):
            part = jnp.dot(all_ref[act_place[s]], w_ref[s, :, cols], preferred_element_type=jnp.float32)
            total = part if total is None else total + part
        return total

    def forward():
        def body(tile, carry):
            cols = pl.ds(pl.multiple_of(tile * TILE, TILE), TILE)
            pre = product(x_all, wu, cols)
            th = jnp.tanh(ROOT * (pre + CUBE * pre * pre * pre))
            hidden[:, cols] = (0.5 * pre * (1.0 + th)).astype(jnp.bfloat16)
            inner = ROOT * (1.0 + 3.0 * CUBE * pre * pre)
            slope[:, cols] = 0.5 * (1.0 + th) + 0.5 * pre * (1.0 - th * th) * inner
            return carry
        lax.fori_loop(0, HB // TILE, body, 0)

    def backward():
        def body(tile, carry):
            cols = pl.ds(pl.multiple_of(tile * TILE, TILE), TILE)
            gpre[:, cols] = (product(c_all, wd, cols) * slope[:, cols]).astype(jnp.bfloat16)
            return carry
        lax.fori_loop(0, HB // TILE, body, 0)

    def term(o, s):
        act_ref, w_ref = ((hidden, wd), (gpre, wu))[o]
        total = lax.dot_general(
            act_ref[...], w_ref[s], (((1,), (1,)), ((), ())), preferred_element_type=jnp.float32)
        if s in (0, 3):
            terms[o, s // 3] = total
        else:
            sendbuf[o, s] = total.astype(jnp.bfloat16)

    first_slot = [[sends.slot() for _ in range(2)] for _ in range(2)]
    last_slot = [[sends.slot() for _ in range(2)] for _ in range(2)]
    sum_group = [sends.group() for _ in range(2)]
    out_slot = [sends.slot() for _ in range(2)]
    out_group = [sends.group() for _ in range(2)]
    sum_rows = (sib_rows, own_rows)
    outs = (out_mixed, out_grad)
    last = []

    def sum_send(o, ch, s, place, slot, device):
        rows = sum_rows[ch]
        sends.start(sendbuf.at[o, s, rows, :], landed.at[o, place, rows, :], sum_group[o], slot[o][ch], device)

    def sum_eight(o, ch):
        sum_send(o, ch, 4, 3, first_slot, along(d4 + d8))

    def near_two(o, ch):
        sum_send(o, ch, 2, 1, last_slot, along(d2))

    def near_one(o, ch):
        sum_send(o, ch, 1, 0, last_slot, along(d1))

    def near_four(o, ch):
        rows = sum_rows[ch]
        sends.arrive(landed.at[o, 3, rows, :], first_slot[o][ch], sibling)
        total = terms[o, 1, rows, :] + landed[o, 3, rows, :].astype(jnp.float32)
        sendbuf[o, 3, rows, :] = total.astype(jnp.bfloat16)
        sum_send(o, ch, 3, 2, last_slot, along(d4))

    def near_sum(o, ch):
        rows = sum_rows[ch]
        sends.arrive(landed.at[o, 0:3, rows, :], last_slot[o][ch], sibling)
        total = terms[o, 0, rows, :]
        for place in range(3):
            total = total + landed[o, place, rows, :].astype(jnp.float32)
        sendbuf[o, 0, rows, :] = total.astype(jnp.bfloat16)
        if ch == 0:
            sends.start(sendbuf.at[o, 0, sib_rows, :], outs[o].at[:, mine], out_group[o], out_slot[o], sibling)
        else:
            copy = pltpu.make_async_copy(sendbuf.at[o, 0, own_rows, :], outs[o].at[:, mine], local_sem.at[4 + o])
            copy.start()
            last.append(copy)

    T, C, M, G = 0, 1, 0, 1
    UP, DA, DB = 0, 1, 2
    near_own(T,0)
    w_join(0)
    w_start(0)
    near_own(T,1)
    w_join(1)
    w_start(1)
    w_near(0)
    w_pass(0, 0)
    act_four(T,0)
    w_far(0)
    w_start(2)
    act_four(T,1)
    near_own(C,0)
    near_own(C,1)
    w_near(1)
    w_pass(0, 1)
    w_pass(0, 2)
    w_pass(1, 0)
    w_pass(0, 3)
    w_far(1)
    w_near(2)
    w_pass(1, 1)
    w_pass(1, 2)
    w_end(0)
    w_pass(2, 0)
    w_far(2)
    w_pass(1, 3)
    act_four(C,0)
    w_end(1)
    near_end(T,0)
    near_end(T,1)
    forward()
    term(M,4)
    sum_eight(M,0)
    sum_eight(M,1)
    w_pass(2, 1)
    w_pass(2, 2)
    w_pass(2, 3)
    w_end(2)
    act_four(C,1)
    term(M,2)
    near_two(M,0)
    term(M,3)
    near_four(M,0)
    term(M,1)
    near_two(M,1)
    near_one(M,0)
    near_four(M,1)
    near_one(M,1)
    term(M,0)
    near_end(C,0)
    near_end(C,1)
    backward()
    term(G,4)
    sum_eight(G,0)
    sum_eight(G,1)
    term(G,2)
    near_two(G,0)
    term(G,3)
    near_four(G,0)
    near_two(G,1)
    near_four(G,1)
    term(G,1)
    near_one(G,0)
    near_one(G,1)
    term(G,0)
    near_sum(M,0)
    near_sum(M,1)
    near_sum(G,0)
    near_sum(G,1)
    for o in range(2):
        sends.arrive(outs[o].at[:, theirs], out_slot[o], sibling)
    for copy in last:
        copy.wait()
    for n in range(2):
        sends.left(alls[n].at[0, own_rows, :], swap_act_group[n], sibling)
        sends.left(stage.at[n, 1], swap_w_group[n], sibling)
        sends.left(alls[n].at[0:4], act_group[n], sibling)
        sends.left(sendbuf.at[n, 0:4], sum_group[n], sibling)
        sends.left(sendbuf.at[n, 0, sib_rows, :], out_group[n], sibling)
    for n, (array, first, end) in enumerate(parts):
        sends.left(gathered[array].at[first:end, 0:240, :], w_group[n], sibling)
    assert sends.groups == SEND_SEMS and sends.received == RECV_SEMS


def on_device(tokens, cotangent, up_weight, down_weight):
    any_spec = pl.BlockSpec(memory_space=pl.ANY)
    hbm_spec = pl.BlockSpec(memory_space=pltpu.HBM)
    bf, f32 = jnp.bfloat16, jnp.float32
    return pl.pallas_call(
        kernel,
        out_shape=[jax.ShapeDtypeStruct(tokens.shape, bf)] * 2,
        in_specs=[hbm_spec] * 4,
        out_specs=[any_spec] * 2,
        scratch_shapes=[
            pltpu.VMEM((TERMS, 2 * TOK, BLK), bf),
            pltpu.VMEM((TERMS, 2 * TOK, BLK), bf),
            pltpu.VMEM((TERMS, BLK, HB), bf),
            pltpu.VMEM((TERMS, BLK, HB), bf),
            pltpu.VMEM((2, 2, TERMS, 8, HB), bf),
            pltpu.VMEM((2, 2, 2 * TOK, BLK), f32),
            pltpu.VMEM((2, TERMS, 2 * TOK, BLK), bf),
            pltpu.VMEM((2, 4, 2 * TOK, BLK), bf),
            pltpu.VMEM((2 * TOK, HB), bf),
            pltpu.VMEM((2 * TOK, HB), f32),
            pltpu.VMEM((2 * TOK, HB), bf),
            pltpu.SemaphoreType.DMA((6,)),
            pltpu.SemaphoreType.DMA((SEND_SEMS,)),
            pltpu.SemaphoreType.DMA((RECV_SEMS,)),
        ],
        compiler_params=pltpu.CompilerParams(
            collective_id=0, has_side_effects=True, vmem_limit_bytes=48 * 1024 * 1024),
    )(*[pltpu.with_memory_space_constraint(v, pltpu.HBM) for v in (tokens, cotangent, up_weight, down_weight)])


def solution(mesh):
    act, weight = P("dp", "mp"), P(None, "dp", "mp")
    return jax.shard_map(
        on_device, mesh=mesh, in_specs=(act, act, weight, weight), out_specs=(act, act), check_vma=False)
```

```python
import math

import jax
import jax.numpy as jnp
from jax import lax
from jax.experimental import pallas as pl
from jax.experimental.pallas import tpu as pltpu
from jax.sharding import PartitionSpec as P

BLK = 256
TERMS = 5
HB = 1024
TOK = 128
SIDE = 4
MESH = pl.DeviceIdType.MESH
ROOT = math.sqrt(2.0 / math.pi)
CUBE = 0.044715
SEND_SEMS, RECV_SEMS = 13, 66


def xor_step(bit, amount):
    return amount - 2 * amount * bit


class Sends:
    def __init__(self, send_sem, recv_sem):
        self.send_sem, self.recv_sem = send_sem, recv_sem
        self.groups, self.received = 0, 0

    def group(self):
        self.groups += 1
        return self.groups - 1

    def slot(self):
        self.received += 1
        return self.received - 1

    def start(self, src, dst, group, slot, device):
        pltpu.make_async_remote_copy(
            src_ref=src, dst_ref=dst, send_sem=self.send_sem.at[group],
            recv_sem=self.recv_sem.at[slot], device_id=device, device_id_type=MESH,
        ).start()

    def arrive(self, dst, slot, device):
        pltpu.make_async_remote_copy(
            src_ref=dst, dst_ref=dst, send_sem=self.send_sem.at[0],
            recv_sem=self.recv_sem.at[slot], device_id=device, device_id_type=MESH,
        ).wait_recv()

    def left(self, src, group, device):
        pltpu.make_async_remote_copy(
            src_ref=src, dst_ref=src, send_sem=self.send_sem.at[group],
            recv_sem=self.recv_sem.at[0], device_id=device, device_id_type=MESH,
        ).wait_send()


def kernel(tok, cot, up, down, both,
           x_all, c_all, wu, wd, stage, terms, sendbuf, landed, hidden, slope, gpre,
           local_sem, send_sem, recv_sem):
    dp = lax.axis_index("dp")
    z = lax.axis_index("mp")
    core = lax.rem(dp, 2)
    chip = lax.div(dp, 2)
    px, py = lax.rem(chip, SIDE), lax.div(chip, SIDE)
    a = px * (1 - core) + py * core
    b = py * (1 - core) + px * core

    def chip_at(a_pos, b_pos):
        return a_pos * (1 + 3 * core) + b_pos * (4 - 3 * core)

    def ring(pos, step):
        return lax.rem(pos + step + SIDE, SIDE)

    def plane(a_pos, b_pos):
        return (chip_at(a_pos, b_pos) * 2 + core, z)

    b0 = lax.rem(z, 2)
    b1 = lax.rem(lax.div(z, 2), 2)
    b2 = lax.rem(lax.div(z, 4), 2)
    b3 = lax.rem(lax.div(z, 8), 2)
    d1, d2, d4, d8 = xor_step(b0, 1), xor_step(b1, 2), xor_step(b2, 4), xor_step(b3, 8)

    def along(step):
        return (dp, z + step)

    sibling = (dp + 1 - 2 * core, z)
    sends = Sends(send_sem, recv_sem)

    mine = pl.ds(pl.multiple_of(core * BLK, BLK), BLK)
    theirs = pl.ds(pl.multiple_of((1 - core) * BLK, BLK), BLK)
    own_rows = pl.ds(pl.multiple_of(core * TOK, TOK), TOK)
    sib_rows = pl.ds(pl.multiple_of((1 - core) * TOK, TOK), TOK)
    cuts = (1, 1, 2, 2)

    def pieces(base, count):
        step = TOK // count
        return [pl.ds(pl.multiple_of(base * TOK + i * step, step), step) for i in range(count)]

    own_units = pl.ds(pl.multiple_of(core * HB, HB), HB)
    sib_units = pl.ds(pl.multiple_of((1 - core) * HB, HB), HB)
    acts, alls = (tok, cot), (x_all, c_all)
    weights, gathered = (up, down), (wu, wd)

    barrier = pltpu.get_barrier_semaphore()
    a_up, a_down, b_up, b_down = (
        plane(ring(a, 1), b), plane(ring(a, -1), b), plane(a, ring(b, 1)), plane(a, ring(b, -1)))
    greet = [along(s) for s in (d4 + d8, d4, d2, d1)]
    greet += [a_up, a_down, b_up, b_down, sibling]
    for device in greet:
        pl.semaphore_signal(barrier, inc=1, device_id=device, device_id_type=MESH)
    local = []
    for n in range(2):
        local.append(pltpu.make_async_copy(acts[n].at[:, mine], alls[n].at[0, own_rows, :], local_sem.at[n]))
        local.append(pltpu.make_async_copy(weights[n].at[:, :, own_units], stage.at[n, 0], local_sem.at[2 + n]))
    for copy in local:
        copy.start()

    pl.semaphore_wait(barrier, len(greet))

    swap_act = [sends.slot() for _ in range(2)]
    swap_w = [sends.slot() for _ in range(2)]
    swap_act_group = [sends.group() for _ in range(2)]
    swap_w_group = [sends.group() for _ in range(2)]
    for n in range(2):
        sends.start(acts[n].at[:, theirs], alls[n].at[0, own_rows, :], swap_act_group[n], swap_act[n], sibling)
        sends.start(weights[n].at[:, :, sib_units], stage.at[n, 1], swap_w_group[n], swap_w[n], sibling)

    act_rows = [pieces(core, cuts[n]) + pieces(1 - core, cuts[n]) for n in range(2)]
    near_slot = [[sends.slot() for _ in rows] for rows in act_rows]
    four_slot = [[sends.slot() for _ in rows] for rows in act_rows]
    act_group = [sends.group() for _ in range(2)]
    act_place = (0, 1, 2, 4, 3)

    def act_send(n, ch, src, dst, slot, device):
        rows = act_rows[n][ch]
        sends.start(alls[n].at[src, rows, :], alls[n].at[dst, rows, :], act_group[n], slot[n][ch], device)

    def act_four(n, ch):
        sends.arrive(alls[n].at[4, act_rows[n][ch], :], four_slot[n][ch], sibling)
        act_send(n, ch, 4, 3, near_slot, along(d4 + d8))

    def near_own(n, ch):
        if ch == 0:
            local[2 * n].wait()
        elif ch == cuts[n]:
            sends.arrive(alls[n].at[0, sib_rows, :], swap_act[n], sibling)
        act_send(n, ch, 0, 4, four_slot, along(d4))
        act_send(n, ch, 0, 2, near_slot, along(d2))
        act_send(n, ch, 0, 1, near_slot, along(d1))

    def near_end(n, ch):
        sends.arrive(alls[n].at[1:4, act_rows[n][ch], :], near_slot[n][ch], sibling)

    parts = ((0, 0, 5), (1, 3, 5), (1, 0, 3))
    w_slot = [[sends.slot() for _ in range(12)] for _ in parts]
    w_group = [sends.group() for _ in parts]
    ks = (a, ring(a, -1), ring(a, 1), ring(a, 2))
    lo, hi, whole = pl.ds(0, HB // 2), pl.ds(HB // 2, HB // 2), pl.ds(0, HB)

    def piece(n, a_pos, b_pos, cols):
        rows = pl.ds(pl.multiple_of(chip_at(a_pos, b_pos) * 16, 16), 16)
        array, first, end = parts[n]
        return gathered[array].at[first:end, rows, cols]

    def w_send(n, a_pos, b_pos, cols, slot, device):
        ref = piece(n, a_pos, b_pos, cols)
        sends.start(ref, ref, w_group[n], w_slot[n][slot], device)

    def w_wait(n, a_pos, b_pos, slot):
        sends.arrive(piece(n, a_pos, b_pos, whole), w_slot[n][slot], sibling)

    def w_across(n, k):
        w_send(n, ks[k], b, whole, 3 + k, b_up)
        w_send(n, ks[k], b, whole, 7 + k, b_down)

    def w_join(array):
        local[2 * array + 1].wait()
        sends.arrive(stage.at[array, 1], swap_w[array], sibling)
        first = stage[array, 0].astype(jnp.float32)
        second = stage[array, 1].astype(jnp.float32)
        rows = pl.ds(pl.multiple_of(chip * 16, 16), 16)

        @pl.when(core == 0)
        def _():
            gathered[array][:, rows, :] = jnp.concatenate([first, second], axis=1).astype(jnp.bfloat16)

        @pl.when(core == 1)
        def _():
            gathered[array][:, rows, :] = jnp.concatenate([second, first], axis=1).astype(jnp.bfloat16)

    def w_start(n):
        w_send(n, a, b, whole, 0, a_up)
        w_send(n, a, b, whole, 1, a_down)
        w_across(n, 0)

    def w_near(n):
        w_wait(n, ks[1], b, 0)
        w_send(n, ks[1], b, lo, 2, a_up)
        w_wait(n, ks[2], b, 1)
        w_send(n, ks[2], b, hi, 2, a_down)
        w_across(n, 1)
        w_across(n, 2)

    def w_far(n):
        w_wait(n, ks[3], b, 2)
        w_across(n, 3)

    def w_pass(n, k):
        w_wait(n, ks[k], ring(b, -1), 3 + k)
        w_send(n, ks[k], ring(b, -1), lo, 11, b_up)
        w_wait(n, ks[k], ring(b, 1), 7 + k)
        w_send(n, ks[k], ring(b, 1), hi, 11, b_down)

    def w_end(n):
        array, first, end = parts[n]
        sends.arrive(gathered[array].at[first:end, 0:64, :], w_slot[n][11], sibling)

    TILE = 256

    def product(all_ref, w_ref, cols):
        total = None
        for s in range(TERMS):
            part = jnp.dot(all_ref[act_place[s]], w_ref[s, :, cols], preferred_element_type=jnp.float32)
            total = part if total is None else total + part
        return total

    def forward():
        def body(tile, carry):
            cols = pl.ds(pl.multiple_of(tile * TILE, TILE), TILE)
            pre = product(x_all, wu, cols)
            th = jnp.tanh(ROOT * (pre + CUBE * pre * pre * pre))
            hidden[:, cols] = (0.5 * pre * (1.0 + th)).astype(jnp.bfloat16)
            inner = ROOT * (1.0 + 3.0 * CUBE * pre * pre)
            slope[:, cols] = 0.5 * (1.0 + th) + 0.5 * pre * (1.0 - th * th) * inner
            return carry
        lax.fori_loop(0, HB // TILE, body, 0)

    def backward():
        def body(tile, carry):
            cols = pl.ds(pl.multiple_of(tile * TILE, TILE), TILE)
            gpre[:, cols] = (product(c_all, wd, cols) * slope[:, cols]).astype(jnp.bfloat16)
            return carry
        lax.fori_loop(0, HB // TILE, body, 0)

    def term(o, s):
        act_ref, w_ref = ((hidden, wd), (gpre, wu))[o]
        total = lax.dot_general(
            act_ref[...], w_ref[s], (((1,), (1,)), ((), ())), preferred_element_type=jnp.float32)
        if s in (0, 3):
            terms[o, s // 3] = total
        else:
            sendbuf[o, s] = total.astype(jnp.bfloat16)

    sum_rows = [pieces(1 - core, cuts[2 + o]) + pieces(core, cuts[2 + o]) for o in range(2)]
    first_slot = [[sends.slot() for _ in rows] for rows in sum_rows]
    last_slot = [[sends.slot() for _ in rows] for rows in sum_rows]
    sum_group = [sends.group() for _ in range(2)]
    out_slot = [sends.slot() for _ in range(2)]
    out_group = [sends.group() for _ in range(2)]
    outs = (both.at[0], both.at[1])
    last = []

    def sum_send(o, ch, s, place, slot, device):
        rows = sum_rows[o][ch]
        sends.start(sendbuf.at[o, s, rows, :], landed.at[o, place, rows, :], sum_group[o], slot[o][ch], device)

    def sum_eight(o, ch):
        sum_send(o, ch, 4, 3, first_slot, along(d4 + d8))

    def near_two(o, ch):
        sum_send(o, ch, 2, 1, last_slot, along(d2))

    def near_one(o, ch):
        sum_send(o, ch, 1, 0, last_slot, along(d1))

    def near_four(o, ch):
        rows = sum_rows[o][ch]
        sends.arrive(landed.at[o, 3, rows, :], first_slot[o][ch], sibling)
        total = terms[o, 1, rows, :] + landed[o, 3, rows, :].astype(jnp.float32)
        sendbuf[o, 3, rows, :] = total.astype(jnp.bfloat16)
        sum_send(o, ch, 3, 2, last_slot, along(d4))

    def near_sum(o, ch):
        rows = sum_rows[o][ch]
        sends.arrive(landed.at[o, 0:3, rows, :], last_slot[o][ch], sibling)
        total = terms[o, 0, rows, :]
        for place in range(3):
            total = total + landed[o, place, rows, :].astype(jnp.float32)
        sendbuf[o, 0, rows, :] = total.astype(jnp.bfloat16)
        here = pl.ds(ch % cuts[2 + o] * (TOK // cuts[2 + o]), TOK // cuts[2 + o])
        place = outs[o].at[here, mine]
        if ch < cuts[2 + o]:
            sends.start(sendbuf.at[o, 0, rows, :], place, out_group[o], out_slot[o], sibling)
        else:
            copy = pltpu.make_async_copy(sendbuf.at[o, 0, rows, :], place, local_sem.at[4 + 2 * o + ch % cuts[2 + o]])
            copy.start()
            last.append(copy)

    T, C, M, G = 0, 1, 0, 1
    UP, DA, DB = 0, 1, 2
    near_own(T, 0)
    w_join(0)
    w_start(0)
    near_own(T, 1)
    w_join(1)
    w_start(1)
    w_near(0)
    w_pass(0, 0)
    act_four(T, 0)
    w_far(0)
    w_start(2)
    act_four(T, 1)
    near_own(C, 0)
    near_own(C, 1)
    w_near(1)
    w_pass(0, 1)
    w_pass(0, 2)
    w_pass(1, 0)
    w_pass(0, 3)
    w_far(1)
    w_near(2)
    w_pass(1, 1)
    w_pass(1, 2)
    w_end(0)
    w_pass(2, 0)
    w_far(2)
    w_pass(1, 3)
    act_four(C, 0)
    w_end(1)
    near_end(T, 0)
    near_end(T, 1)
    forward()
    term(M,4)
    sum_eight(M, 0)
    sum_eight(M, 1)
    sum_eight(M, 2)
    sum_eight(M, 3)
    w_pass(2, 1)
    w_pass(2, 2)
    w_pass(2, 3)
    w_end(2)
    act_four(C, 1)
    term(M,2)
    near_two(M, 0)
    near_two(M, 1)
    term(M,3)
    near_four(M, 0)
    near_four(M, 1)
    term(M,1)
    near_two(M, 2)
    near_two(M, 3)
    near_one(M, 0)
    near_one(M, 1)
    near_four(M, 2)
    near_four(M, 3)
    near_one(M, 2)
    near_one(M, 3)
    term(M,0)
    near_end(C, 0)
    near_end(C, 1)
    backward()
    term(G,4)
    sum_eight(G, 0)
    sum_eight(G, 1)
    sum_eight(G, 2)
    sum_eight(G, 3)
    term(G,2)
    near_two(G, 0)
    near_two(G, 1)
    term(G,3)
    near_four(G, 0)
    near_four(G, 1)
    near_two(G, 2)
    near_two(G, 3)
    near_four(G, 2)
    near_four(G, 3)
    term(G,1)
    near_one(G, 0)
    near_one(G, 1)
    near_one(G, 2)
    near_one(G, 3)
    term(G,0)
    near_sum(M, 0)
    near_sum(M, 1)
    near_sum(M, 2)
    near_sum(M, 3)
    near_sum(G, 0)
    near_sum(G, 1)
    near_sum(G, 2)
    near_sum(G, 3)
    for o in range(2):
        sends.arrive(outs[o].at[:, theirs], out_slot[o], sibling)
    for copy in last:
        copy.wait()
    for n in range(2):
        sends.left(alls[n].at[0, own_rows, :], swap_act_group[n], sibling)
        sends.left(stage.at[n, 1], swap_w_group[n], sibling)
        sends.left(alls[n].at[0:4], act_group[n], sibling)
        sends.left(sendbuf.at[n, 0:4], sum_group[n], sibling)
        sends.left(sendbuf.at[n, 0, sib_rows, :], out_group[n], sibling)
    for n, (array, first, end) in enumerate(parts):
        sends.left(gathered[array].at[first:end, 0:240, :], w_group[n], sibling)


def on_device(tokens, cotangent, up_weight, down_weight):
    any_spec = pl.BlockSpec(memory_space=pl.ANY)
    hbm_spec = pl.BlockSpec(memory_space=pltpu.HBM)
    bf, f32 = jnp.bfloat16, jnp.float32
    both = pl.pallas_call(
        kernel,
        out_shape=jax.ShapeDtypeStruct((2,) + tokens.shape, bf),
        in_specs=[hbm_spec] * 4,
        out_specs=any_spec,
        scratch_shapes=[
            pltpu.VMEM((TERMS, 2 * TOK, BLK), bf),
            pltpu.VMEM((TERMS, 2 * TOK, BLK), bf),
            pltpu.VMEM((TERMS, BLK, HB), bf),
            pltpu.VMEM((TERMS, BLK, HB), bf),
            pltpu.VMEM((2, 2, TERMS, 8, HB), bf),
            pltpu.VMEM((2, 2, 2 * TOK, BLK), f32),
            pltpu.VMEM((2, TERMS, 2 * TOK, BLK), bf),
            pltpu.VMEM((2, 4, 2 * TOK, BLK), bf),
            pltpu.VMEM((2 * TOK, HB), bf),
            pltpu.VMEM((2 * TOK, HB), f32),
            pltpu.VMEM((2 * TOK, HB), bf),
            pltpu.SemaphoreType.DMA((8,)),
            pltpu.SemaphoreType.DMA((SEND_SEMS,)),
            pltpu.SemaphoreType.DMA((RECV_SEMS,)),
        ],
        compiler_params=pltpu.CompilerParams(
            collective_id=0, has_side_effects=True, vmem_limit_bytes=48 * 1024 * 1024),
    )(*[pltpu.with_memory_space_constraint(v, pltpu.HBM) for v in (tokens, cotangent, up_weight, down_weight)])
    return both[0], both[1]


def solution(mesh):
    act, weight = P("dp", "mp"), P(None, "dp", "mp")
    return jax.shard_map(
        on_device, mesh=mesh, in_specs=(act, act, weight, weight), out_specs=(act, act), check_vma=False)
```

```python
import math

import jax
import jax.numpy as jnp
from jax import lax
from jax.experimental import pallas as pl
from jax.experimental.pallas import tpu as pltpu
from jax.sharding import PartitionSpec as P

BLK = 256
TERMS = 5
HB = 1024
TOK = 128
SIDE = 4
MESH = pl.DeviceIdType.MESH
ROOT = math.sqrt(2.0 / math.pi)
CUBE = 0.044715
SEND_SEMS, RECV_SEMS = 13, 66


def xor_step(bit, amount):
    return amount - 2 * amount * bit


class Sends:
    def __init__(self, send_sem, recv_sem):
        self.send_sem, self.recv_sem = send_sem, recv_sem
        self.groups, self.received = 0, 0

    def group(self):
        self.groups += 1
        return self.groups - 1

    def slot(self):
        self.received += 1
        return self.received - 1

    def start(self, src, dst, group, slot, device):
        pltpu.make_async_remote_copy(
            src_ref=src, dst_ref=dst, send_sem=self.send_sem.at[group],
            recv_sem=self.recv_sem.at[slot], device_id=device, device_id_type=MESH,
        ).start()

    def arrive(self, dst, slot, device):
        pltpu.make_async_remote_copy(
            src_ref=dst, dst_ref=dst, send_sem=self.send_sem.at[0],
            recv_sem=self.recv_sem.at[slot], device_id=device, device_id_type=MESH,
        ).wait_recv()

    def left(self, src, group, device):
        pltpu.make_async_remote_copy(
            src_ref=src, dst_ref=src, send_sem=self.send_sem.at[group],
            recv_sem=self.recv_sem.at[0], device_id=device, device_id_type=MESH,
        ).wait_send()


def kernel(tok, cot, up, down, both,
           x_all, c_all, wu, wd, stage, terms, sendbuf, landed, hidden, slope, gpre,
           local_sem, send_sem, recv_sem):
    dp = lax.axis_index("dp")
    z = lax.axis_index("mp")
    core = lax.rem(dp, 2)
    chip = lax.div(dp, 2)
    px, py = lax.rem(chip, SIDE), lax.div(chip, SIDE)
    a = px * (1 - core) + py * core
    b = py * (1 - core) + px * core

    def chip_at(a_pos, b_pos):
        return a_pos * (1 + 3 * core) + b_pos * (4 - 3 * core)

    def ring(pos, step):
        return lax.rem(pos + step + SIDE, SIDE)

    def plane(a_pos, b_pos):
        return (chip_at(a_pos, b_pos) * 2 + core, z)

    b0 = lax.rem(z, 2)
    b1 = lax.rem(lax.div(z, 2), 2)
    b2 = lax.rem(lax.div(z, 4), 2)
    b3 = lax.rem(lax.div(z, 8), 2)
    d1, d2, d4, d8 = xor_step(b0, 1), xor_step(b1, 2), xor_step(b2, 4), xor_step(b3, 8)

    def along(step):
        return (dp, z + step)

    sibling = (dp + 1 - 2 * core, z)
    sends = Sends(send_sem, recv_sem)

    mine = pl.ds(pl.multiple_of(core * BLK, BLK), BLK)
    theirs = pl.ds(pl.multiple_of((1 - core) * BLK, BLK), BLK)
    own_rows = pl.ds(pl.multiple_of(core * TOK, TOK), TOK)
    sib_rows = pl.ds(pl.multiple_of((1 - core) * TOK, TOK), TOK)
    cuts = (1, 1, 2, 2)

    def pieces(base, count):
        step = TOK // count
        return [pl.ds(pl.multiple_of(base * TOK + i * step, step), step) for i in range(count)]

    own_units = pl.ds(pl.multiple_of(core * HB, HB), HB)
    sib_units = pl.ds(pl.multiple_of((1 - core) * HB, HB), HB)
    acts, alls = (tok, cot), (x_all, c_all)
    weights, gathered = (up, down), (wu, wd)

    barrier = pltpu.get_barrier_semaphore()
    a_up, a_down, b_up, b_down = (
        plane(ring(a, 1), b), plane(ring(a, -1), b), plane(a, ring(b, 1)), plane(a, ring(b, -1)))
    greet = [along(s) for s in (d4 + d8, d4, d2, d1)]
    greet += [a_up, a_down, b_up, b_down, sibling]
    for device in greet:
        pl.semaphore_signal(barrier, inc=1, device_id=device, device_id_type=MESH)
    local = []
    for n in range(2):
        local.append(pltpu.make_async_copy(acts[n].at[:, mine], alls[n].at[0, own_rows, :], local_sem.at[n]))
        local.append(pltpu.make_async_copy(weights[n].at[:, :, own_units], stage.at[n, 0], local_sem.at[2 + n]))
    for copy in local:
        copy.start()

    pl.semaphore_wait(barrier, len(greet))

    swap_act = [sends.slot() for _ in range(2)]
    swap_w = [sends.slot() for _ in range(2)]
    swap_act_group = [sends.group() for _ in range(2)]
    swap_w_group = [sends.group() for _ in range(2)]
    for n in range(2):
        sends.start(acts[n].at[:, theirs], alls[n].at[0, own_rows, :], swap_act_group[n], swap_act[n], sibling)
        sends.start(weights[n].at[:, :, sib_units], stage.at[n, 1], swap_w_group[n], swap_w[n], sibling)

    act_rows = [pieces(core, cuts[n]) + pieces(1 - core, cuts[n]) for n in range(2)]
    near_slot = [[sends.slot() for _ in rows] for rows in act_rows]
    four_slot = [[sends.slot() for _ in rows] for rows in act_rows]
    act_group = [sends.group() for _ in range(2)]
    act_place = (0, 1, 2, 4, 3)

    def act_send(n, ch, src, dst, slot, device):
        rows = act_rows[n][ch]
        sends.start(alls[n].at[src, rows, :], alls[n].at[dst, rows, :], act_group[n], slot[n][ch], device)

    def act_four(n, ch):
        sends.arrive(alls[n].at[4, act_rows[n][ch], :], four_slot[n][ch], sibling)
        act_send(n, ch, 4, 3, near_slot, along(d4 + d8))

    def near_own(n, ch):
        if ch == 0:
            local[2 * n].wait()
        elif ch == cuts[n]:
            sends.arrive(alls[n].at[0, sib_rows, :], swap_act[n], sibling)
        act_send(n, ch, 0, 4, four_slot, along(d4))
        act_send(n, ch, 0, 2, near_slot, along(d2))
        act_send(n, ch, 0, 1, near_slot, along(d1))

    def near_end(n, ch):
        sends.arrive(alls[n].at[1:4, act_rows[n][ch], :], near_slot[n][ch], sibling)

    parts = ((0, 0, 5), (1, 2, 5), (1, 0, 2))
    w_slot = [[sends.slot() for _ in range(12)] for _ in parts]
    w_group = [sends.group() for _ in parts]
    ks = (a, ring(a, -1), ring(a, 1), ring(a, 2))
    lo, hi, whole = pl.ds(0, HB // 2), pl.ds(HB // 2, HB // 2), pl.ds(0, HB)

    def piece(n, a_pos, b_pos, cols):
        rows = pl.ds(pl.multiple_of(chip_at(a_pos, b_pos) * 16, 16), 16)
        array, first, end = parts[n]
        return gathered[array].at[first:end, rows, cols]

    def w_send(n, a_pos, b_pos, cols, slot, device):
        ref = piece(n, a_pos, b_pos, cols)
        sends.start(ref, ref, w_group[n], w_slot[n][slot], device)

    def w_wait(n, a_pos, b_pos, slot):
        sends.arrive(piece(n, a_pos, b_pos, whole), w_slot[n][slot], sibling)

    def w_across(n, k):
        w_send(n, ks[k], b, whole, 3 + k, b_up)
        w_send(n, ks[k], b, whole, 7 + k, b_down)

    def w_join(array):
        local[2 * array + 1].wait()
        sends.arrive(stage.at[array, 1], swap_w[array], sibling)
        first = stage[array, 0].astype(jnp.float32)
        second = stage[array, 1].astype(jnp.float32)
        rows = pl.ds(pl.multiple_of(chip * 16, 16), 16)

        @pl.when(core == 0)
        def _():
            gathered[array][:, rows, :] = jnp.concatenate([first, second], axis=1).astype(jnp.bfloat16)

        @pl.when(core == 1)
        def _():
            gathered[array][:, rows, :] = jnp.concatenate([second, first], axis=1).astype(jnp.bfloat16)

    def w_start(n):
        w_send(n, a, b, whole, 0, a_up)
        w_send(n, a, b, whole, 1, a_down)
        w_across(n, 0)

    def w_near(n):
        w_wait(n, ks[1], b, 0)
        w_send(n, ks[1], b, lo, 2, a_up)
        w_wait(n, ks[2], b, 1)
        w_send(n, ks[2], b, hi, 2, a_down)
        w_across(n, 1)
        w_across(n, 2)

    def w_far(n):
        w_wait(n, ks[3], b, 2)
        w_across(n, 3)

    def w_pass(n, k):
        w_wait(n, ks[k], ring(b, -1), 3 + k)
        w_send(n, ks[k], ring(b, -1), lo, 11, b_up)
        w_wait(n, ks[k], ring(b, 1), 7 + k)
        w_send(n, ks[k], ring(b, 1), hi, 11, b_down)

    def w_end(n):
        array, first, end = parts[n]
        sends.arrive(gathered[array].at[first:end, 0:64, :], w_slot[n][11], sibling)

    TILE = 256

    def product(all_ref, w_ref, cols):
        total = None
        for s in range(TERMS):
            part = jnp.dot(all_ref[act_place[s]], w_ref[s, :, cols], preferred_element_type=jnp.float32)
            total = part if total is None else total + part
        return total

    def forward():
        def body(tile, carry):
            cols = pl.ds(pl.multiple_of(tile * TILE, TILE), TILE)
            pre = product(x_all, wu, cols)
            th = jnp.tanh(ROOT * (pre + CUBE * pre * pre * pre))
            hidden[:, cols] = (0.5 * pre * (1.0 + th)).astype(jnp.bfloat16)
            inner = ROOT * (1.0 + 3.0 * CUBE * pre * pre)
            slope[:, cols] = 0.5 * (1.0 + th) + 0.5 * pre * (1.0 - th * th) * inner
            return carry
        lax.fori_loop(0, HB // TILE, body, 0)

    def backward():
        def body(tile, carry):
            cols = pl.ds(pl.multiple_of(tile * TILE, TILE), TILE)
            gpre[:, cols] = (product(c_all, wd, cols) * slope[:, cols]).astype(jnp.bfloat16)
            return carry
        lax.fori_loop(0, HB // TILE, body, 0)

    def term(o, s):
        act_ref, w_ref = ((hidden, wd), (gpre, wu))[o]
        total = lax.dot_general(
            act_ref[...], w_ref[s], (((1,), (1,)), ((), ())), preferred_element_type=jnp.float32)
        if s in (0, 3):
            terms[o, s // 3] = total
        else:
            sendbuf[o, s] = total.astype(jnp.bfloat16)

    sum_rows = [pieces(1 - core, cuts[2 + o]) + pieces(core, cuts[2 + o]) for o in range(2)]
    first_slot = [[sends.slot() for _ in rows] for rows in sum_rows]
    last_slot = [[sends.slot() for _ in rows] for rows in sum_rows]
    sum_group = [sends.group() for _ in range(2)]
    out_slot = [sends.slot() for _ in range(2)]
    out_group = [sends.group() for _ in range(2)]
    outs = (both.at[0], both.at[1])
    last = []

    def sum_send(o, ch, s, place, slot, device):
        rows = sum_rows[o][ch]
        sends.start(sendbuf.at[o, s, rows, :], landed.at[o, place, rows, :], sum_group[o], slot[o][ch], device)

    def sum_eight(o, ch):
        sum_send(o, ch, 4, 3, first_slot, along(d4 + d8))

    def near_two(o, ch):
        sum_send(o, ch, 2, 1, last_slot, along(d2))

    def near_one(o, ch):
        sum_send(o, ch, 1, 0, last_slot, along(d1))

    def near_four(o, ch):
        rows = sum_rows[o][ch]
        sends.arrive(landed.at[o, 3, rows, :], first_slot[o][ch], sibling)
        total = terms[o, 1, rows, :] + landed[o, 3, rows, :].astype(jnp.float32)
        sendbuf[o, 3, rows, :] = total.astype(jnp.bfloat16)
        sum_send(o, ch, 3, 2, last_slot, along(d4))

    def near_sum(o, ch):
        rows = sum_rows[o][ch]
        sends.arrive(landed.at[o, 0:3, rows, :], last_slot[o][ch], sibling)
        total = terms[o, 0, rows, :]
        for place in range(3):
            total = total + landed[o, place, rows, :].astype(jnp.float32)
        sendbuf[o, 0, rows, :] = total.astype(jnp.bfloat16)
        here = pl.ds(ch % cuts[2 + o] * (TOK // cuts[2 + o]), TOK // cuts[2 + o])
        place = outs[o].at[here, mine]
        if ch < cuts[2 + o]:
            sends.start(sendbuf.at[o, 0, rows, :], place, out_group[o], out_slot[o], sibling)
        else:
            copy = pltpu.make_async_copy(sendbuf.at[o, 0, rows, :], place, local_sem.at[4 + 2 * o + ch % cuts[2 + o]])
            copy.start()
            last.append(copy)

    T, C, M, G = 0, 1, 0, 1
    UP, DA, DB = 0, 1, 2
    near_own(T, 0)
    w_join(0)
    w_start(0)
    near_own(T, 1)
    w_join(1)
    w_start(1)
    w_near(0)
    w_pass(0, 0)
    act_four(T, 0)
    w_far(0)
    w_start(2)
    act_four(T, 1)
    near_own(C, 0)
    near_own(C, 1)
    w_near(1)
    w_pass(0, 1)
    w_pass(0, 2)
    w_pass(1, 0)
    w_pass(0, 3)
    w_far(1)
    w_near(2)
    w_pass(1, 1)
    w_pass(1, 2)
    w_end(0)
    w_pass(2, 0)
    w_far(2)
    w_pass(1, 3)
    act_four(C, 0)
    w_end(1)
    near_end(T, 0)
    near_end(T, 1)
    forward()
    term(M,4)
    sum_eight(M, 0)
    sum_eight(M, 1)
    sum_eight(M, 2)
    sum_eight(M, 3)
    term(M,2)
    near_two(M, 0)
    near_two(M, 1)
    near_two(M, 2)
    near_two(M, 3)
    w_pass(2, 1)
    act_four(C, 1)
    w_pass(2, 2)
    w_pass(2, 3)
    w_end(2)
    term(M,3)
    near_four(M, 0)
    near_four(M, 1)
    term(M,1)
    near_one(M, 0)
    near_one(M, 1)
    near_four(M, 2)
    near_four(M, 3)
    near_one(M, 2)
    near_one(M, 3)
    term(M,0)
    near_end(C, 0)
    near_end(C, 1)
    backward()
    term(G,4)
    sum_eight(G, 0)
    sum_eight(G, 1)
    sum_eight(G, 2)
    sum_eight(G, 3)
    term(G,2)
    near_two(G, 0)
    near_two(G, 1)
    term(G,3)
    near_four(G, 0)
    near_four(G, 1)
    near_two(G, 2)
    near_two(G, 3)
    near_four(G, 2)
    near_four(G, 3)
    term(G,1)
    near_one(G, 0)
    near_one(G, 1)
    near_one(G, 2)
    near_one(G, 3)
    term(G,0)
    near_sum(M, 0)
    near_sum(M, 1)
    near_sum(M, 2)
    near_sum(M, 3)
    near_sum(G, 0)
    near_sum(G, 1)
    near_sum(G, 2)
    near_sum(G, 3)
    for o in range(2):
        sends.arrive(outs[o].at[:, theirs], out_slot[o], sibling)
    for copy in last:
        copy.wait()
    for n in range(2):
        sends.left(alls[n].at[0, own_rows, :], swap_act_group[n], sibling)
        sends.left(stage.at[n, 1], swap_w_group[n], sibling)
        sends.left(alls[n].at[0:4], act_group[n], sibling)
        sends.left(sendbuf.at[n, 0:4], sum_group[n], sibling)
        sends.left(sendbuf.at[n, 0, sib_rows, :], out_group[n], sibling)
    for n, (array, first, end) in enumerate(parts):
        sends.left(gathered[array].at[first:end, 0:240, :], w_group[n], sibling)


def on_device(tokens, cotangent, up_weight, down_weight):
    any_spec = pl.BlockSpec(memory_space=pl.ANY)
    hbm_spec = pl.BlockSpec(memory_space=pltpu.HBM)
    bf, f32 = jnp.bfloat16, jnp.float32
    both = pl.pallas_call(
        kernel,
        out_shape=jax.ShapeDtypeStruct((2,) + tokens.shape, bf),
        in_specs=[hbm_spec] * 4,
        out_specs=any_spec,
        scratch_shapes=[
            pltpu.VMEM((TERMS, 2 * TOK, BLK), bf),
            pltpu.VMEM((TERMS, 2 * TOK, BLK), bf),
            pltpu.VMEM((TERMS, BLK, HB), bf),
            pltpu.VMEM((TERMS, BLK, HB), bf),
            pltpu.VMEM((2, 2, TERMS, 8, HB), bf),
            pltpu.VMEM((2, 2, 2 * TOK, BLK), f32),
            pltpu.VMEM((2, TERMS, 2 * TOK, BLK), bf),
            pltpu.VMEM((2, 4, 2 * TOK, BLK), bf),
            pltpu.VMEM((2 * TOK, HB), bf),
            pltpu.VMEM((2 * TOK, HB), f32),
            pltpu.VMEM((2 * TOK, HB), bf),
            pltpu.SemaphoreType.DMA((8,)),
            pltpu.SemaphoreType.DMA((SEND_SEMS,)),
            pltpu.SemaphoreType.DMA((RECV_SEMS,)),
        ],
        compiler_params=pltpu.CompilerParams(
            collective_id=0, has_side_effects=True, vmem_limit_bytes=48 * 1024 * 1024),
    )(*[pltpu.with_memory_space_constraint(v, pltpu.HBM) for v in (tokens, cotangent, up_weight, down_weight)])
    return both[0], both[1]


def solution(mesh):
    act, weight = P("dp", "mp"), P(None, "dp", "mp")
    return jax.shard_map(
        on_device, mesh=mesh, in_specs=(act, act, weight, weight), out_specs=(act, act), check_vma=False)
```

```python
import math

import jax
import jax.numpy as jnp
from jax import lax
from jax.experimental import pallas as pl
from jax.experimental.pallas import tpu as pltpu
from jax.sharding import PartitionSpec as P

BLK = 256
TERMS = 5
HB = 1024
TOK = 128
SIDE = 4
MESH = pl.DeviceIdType.MESH
ROOT = math.sqrt(2.0 / math.pi)
CUBE = 0.044715
SEND_SEMS, RECV_SEMS = 13, 54


def xor_step(bit, amount):
    return amount - 2 * amount * bit


class Sends:
    def __init__(self, send_sem, recv_sem):
        self.send_sem, self.recv_sem = send_sem, recv_sem
        self.groups, self.received = 0, 0

    def group(self):
        self.groups += 1
        return self.groups - 1

    def slot(self):
        self.received += 1
        return self.received - 1

    def start(self, src, dst, group, slot, device):
        pltpu.make_async_remote_copy(
            src_ref=src, dst_ref=dst, send_sem=self.send_sem.at[group],
            recv_sem=self.recv_sem.at[slot], device_id=device, device_id_type=MESH,
        ).start()

    def arrive(self, dst, slot, device):
        pltpu.make_async_remote_copy(
            src_ref=dst, dst_ref=dst, send_sem=self.send_sem.at[0],
            recv_sem=self.recv_sem.at[slot], device_id=device, device_id_type=MESH,
        ).wait_recv()

    def left(self, src, group, device):
        pltpu.make_async_remote_copy(
            src_ref=src, dst_ref=src, send_sem=self.send_sem.at[group],
            recv_sem=self.recv_sem.at[0], device_id=device, device_id_type=MESH,
        ).wait_send()


def kernel(tok, cot, up, down, both,
           x_all, c_all, wu, wd, stage, terms, sendbuf, landed, hidden, slope, gpre,
           local_sem, send_sem, recv_sem):
    dp = lax.axis_index("dp")
    z = lax.axis_index("mp")
    core = lax.rem(dp, 2)
    chip = lax.div(dp, 2)
    px, py = lax.rem(chip, SIDE), lax.div(chip, SIDE)
    a = px * (1 - core) + py * core
    b = py * (1 - core) + px * core

    def chip_at(a_pos, b_pos):
        return a_pos * (1 + 3 * core) + b_pos * (4 - 3 * core)

    def ring(pos, step):
        return lax.rem(pos + step + SIDE, SIDE)

    def plane(a_pos, b_pos):
        return (chip_at(a_pos, b_pos) * 2 + core, z)

    b0 = lax.rem(z, 2)
    b1 = lax.rem(lax.div(z, 2), 2)
    b2 = lax.rem(lax.div(z, 4), 2)
    b3 = lax.rem(lax.div(z, 8), 2)
    d1, d2, d4, d8 = xor_step(b0, 1), xor_step(b1, 2), xor_step(b2, 4), xor_step(b3, 8)

    def along(step):
        return (dp, z + step)

    sibling = (dp + 1 - 2 * core, z)
    sends = Sends(send_sem, recv_sem)

    mine = pl.ds(pl.multiple_of(core * BLK, BLK), BLK)
    theirs = pl.ds(pl.multiple_of((1 - core) * BLK, BLK), BLK)
    own_rows = pl.ds(pl.multiple_of(core * TOK, TOK), TOK)
    sib_rows = pl.ds(pl.multiple_of((1 - core) * TOK, TOK), TOK)
    cuts = (1, 1, 2, 2)

    def pieces(base, count):
        step = TOK // count
        return [pl.ds(pl.multiple_of(base * TOK + i * step, step), step) for i in range(count)]

    own_units = pl.ds(pl.multiple_of(core * HB, HB), HB)
    sib_units = pl.ds(pl.multiple_of((1 - core) * HB, HB), HB)
    acts, alls = (tok, cot), (x_all, c_all)
    weights, gathered = (up, down), (wu, wd)

    barrier = pltpu.get_barrier_semaphore()
    a_up, a_down, b_up, b_down = (
        plane(ring(a, 1), b), plane(ring(a, -1), b), plane(a, ring(b, 1)), plane(a, ring(b, -1)))
    greet = [along(s) for s in (d4 + d8, d4, d2, d1)]
    greet += [a_up, a_down, b_up, b_down, sibling]
    for device in greet:
        pl.semaphore_signal(barrier, inc=1, device_id=device, device_id_type=MESH)
    local = []
    for n in range(2):
        local.append(pltpu.make_async_copy(acts[n].at[:, mine], alls[n].at[0, own_rows, :], local_sem.at[n]))
        local.append(pltpu.make_async_copy(weights[n].at[:, :, own_units], stage.at[n, 0], local_sem.at[2 + n]))
    for copy in local:
        copy.start()

    pl.semaphore_wait(barrier, len(greet))

    swap_act = [sends.slot() for _ in range(2)]
    swap_w = [sends.slot() for _ in range(2)]
    swap_act_group = [sends.group() for _ in range(2)]
    swap_w_group = [sends.group() for _ in range(2)]
    for n in range(2):
        sends.start(acts[n].at[:, theirs], alls[n].at[0, own_rows, :], swap_act_group[n], swap_act[n], sibling)
        sends.start(weights[n].at[:, :, sib_units], stage.at[n, 1], swap_w_group[n], swap_w[n], sibling)

    act_rows = [pieces(core, cuts[n]) + pieces(1 - core, cuts[n]) for n in range(2)]
    near_slot = [[sends.slot() for _ in rows] for rows in act_rows]
    four_slot = [[sends.slot() for _ in rows] for rows in act_rows]
    act_group = [sends.group() for _ in range(2)]
    act_place = (0, 1, 2, 4, 3)

    def act_send(n, ch, src, dst, slot, device):
        rows = act_rows[n][ch]
        sends.start(alls[n].at[src, rows, :], alls[n].at[dst, rows, :], act_group[n], slot[n][ch], device)

    def act_four(n, ch):
        sends.arrive(alls[n].at[4, act_rows[n][ch], :], four_slot[n][ch], sibling)
        act_send(n, ch, 4, 3, near_slot, along(d4 + d8))

    def near_own(n, ch):
        if ch == 0:
            local[2 * n].wait()
        elif ch == cuts[n]:
            sends.arrive(alls[n].at[0, sib_rows, :], swap_act[n], sibling)
        act_send(n, ch, 0, 4, four_slot, along(d4))
        act_send(n, ch, 0, 2, near_slot, along(d2))
        act_send(n, ch, 0, 1, near_slot, along(d1))

    def near_end(n, ch):
        sends.arrive(alls[n].at[1:4, act_rows[n][ch], :], near_slot[n][ch], sibling)

    parts = ((0, 0, 5), (1, 2, 5), (1, 0, 2))
    w_slot = [[sends.slot() for _ in range(8)] for _ in parts]
    w_group = [sends.group() for _ in parts]
    ks = (a, ring(a, -1), ring(a, 1), ring(a, 2))
    lo, hi, whole = pl.ds(0, HB // 2), pl.ds(HB // 2, HB // 2), pl.ds(0, HB)

    def piece(n, a_pos, b_pos, cols):
        rows = pl.ds(pl.multiple_of(chip_at(a_pos, b_pos) * 16, 16), 16)
        array, first, end = parts[n]
        return gathered[array].at[first:end, rows, cols]

    def w_send(n, a_pos, b_pos, cols, slot, device):
        ref = piece(n, a_pos, b_pos, cols)
        sends.start(ref, ref, w_group[n], w_slot[n][slot], device)

    def w_wait(n, a_pos, b_pos, slot):
        sends.arrive(piece(n, a_pos, b_pos, whole), w_slot[n][slot], sibling)

    def w_across(n, k):
        w_send(n, ks[k], b, whole, 3 + k, b_up)
        w_send(n, ks[k], b, whole, 3 + k, b_down)

    def w_join(array):
        local[2 * array + 1].wait()
        sends.arrive(stage.at[array, 1], swap_w[array], sibling)
        first = stage[array, 0].astype(jnp.float32)
        second = stage[array, 1].astype(jnp.float32)
        rows = pl.ds(pl.multiple_of(chip * 16, 16), 16)

        @pl.when(core == 0)
        def _():
            gathered[array][:, rows, :] = jnp.concatenate([first, second], axis=1).astype(jnp.bfloat16)

        @pl.when(core == 1)
        def _():
            gathered[array][:, rows, :] = jnp.concatenate([second, first], axis=1).astype(jnp.bfloat16)

    def w_start(n):
        w_send(n, a, b, whole, 0, a_up)
        w_send(n, a, b, whole, 1, a_down)
        w_across(n, 0)

    def w_near(n):
        w_wait(n, ks[1], b, 0)
        w_send(n, ks[1], b, lo, 2, a_up)
        w_wait(n, ks[2], b, 1)
        w_send(n, ks[2], b, hi, 2, a_down)
        w_across(n, 1)
        w_across(n, 2)

    def w_far(n):
        w_wait(n, ks[3], b, 2)
        w_across(n, 3)

    def w_pass(n, k):
        array, first, end = parts[n]
        sends.arrive(gathered[array].at[first:end, 0:32, :], w_slot[n][3 + k], sibling)
        w_send(n, ks[k], ring(b, -1), lo, 7, b_up)
        w_send(n, ks[k], ring(b, 1), hi, 7, b_down)

    def w_end(n):
        array, first, end = parts[n]
        sends.arrive(gathered[array].at[first:end, 0:64, :], w_slot[n][7], sibling)

    TILE = 256

    def product(all_ref, w_ref, cols):
        total = None
        for s in range(TERMS):
            part = jnp.dot(all_ref[act_place[s]], w_ref[s, :, cols], preferred_element_type=jnp.float32)
            total = part if total is None else total + part
        return total

    def forward():
        def body(tile, carry):
            cols = pl.ds(pl.multiple_of(tile * TILE, TILE), TILE)
            pre = product(x_all, wu, cols)
            th = jnp.tanh(ROOT * (pre + CUBE * pre * pre * pre))
            hidden[:, cols] = (0.5 * pre * (1.0 + th)).astype(jnp.bfloat16)
            inner = ROOT * (1.0 + 3.0 * CUBE * pre * pre)
            slope[:, cols] = 0.5 * (1.0 + th) + 0.5 * pre * (1.0 - th * th) * inner
            return carry
        lax.fori_loop(0, HB // TILE, body, 0)

    def backward():
        def body(tile, carry):
            cols = pl.ds(pl.multiple_of(tile * TILE, TILE), TILE)
            gpre[:, cols] = (product(c_all, wd, cols) * slope[:, cols]).astype(jnp.bfloat16)
            return carry
        lax.fori_loop(0, HB // TILE, body, 0)

    def term(o, s):
        act_ref, w_ref = ((hidden, wd), (gpre, wu))[o]
        total = lax.dot_general(
            act_ref[...], w_ref[s], (((1,), (1,)), ((), ())), preferred_element_type=jnp.float32)
        if s in (0, 3):
            terms[o, s // 3] = total
        else:
            sendbuf[o, s] = total.astype(jnp.bfloat16)

    sum_rows = [pieces(1 - core, cuts[2 + o]) + pieces(core, cuts[2 + o]) for o in range(2)]
    first_slot = [[sends.slot() for _ in rows] for rows in sum_rows]
    last_slot = [[sends.slot() for _ in rows] for rows in sum_rows]
    sum_group = [sends.group() for _ in range(2)]
    out_slot = [sends.slot() for _ in range(2)]
    out_group = [sends.group() for _ in range(2)]
    outs = (both.at[0], both.at[1])
    last = []

    def sum_send(o, ch, s, place, slot, device):
        rows = sum_rows[o][ch]
        sends.start(sendbuf.at[o, s, rows, :], landed.at[o, place, rows, :], sum_group[o], slot[o][ch], device)

    def sum_eight(o, ch):
        sum_send(o, ch, 4, 3, first_slot, along(d4 + d8))

    def near_two(o, ch):
        sum_send(o, ch, 2, 1, last_slot, along(d2))

    def near_one(o, ch):
        sum_send(o, ch, 1, 0, last_slot, along(d1))

    def near_four(o, ch):
        rows = sum_rows[o][ch]
        sends.arrive(landed.at[o, 3, rows, :], first_slot[o][ch], sibling)
        total = terms[o, 1, rows, :] + landed[o, 3, rows, :].astype(jnp.float32)
        sendbuf[o, 3, rows, :] = total.astype(jnp.bfloat16)
        sum_send(o, ch, 3, 2, last_slot, along(d4))

    def near_sum(o, ch):
        rows = sum_rows[o][ch]
        sends.arrive(landed.at[o, 0:3, rows, :], last_slot[o][ch], sibling)
        total = terms[o, 0, rows, :]
        for place in range(3):
            total = total + landed[o, place, rows, :].astype(jnp.float32)
        sendbuf[o, 0, rows, :] = total.astype(jnp.bfloat16)
        here = pl.ds(ch % cuts[2 + o] * (TOK // cuts[2 + o]), TOK // cuts[2 + o])
        place = outs[o].at[here, mine]
        if ch < cuts[2 + o]:
            sends.start(sendbuf.at[o, 0, rows, :], place, out_group[o], out_slot[o], sibling)
        else:
            copy = pltpu.make_async_copy(sendbuf.at[o, 0, rows, :], place, local_sem.at[4 + 2 * o + ch % cuts[2 + o]])
            copy.start()
            last.append(copy)

    T, C, M, G = 0, 1, 0, 1
    UP, DA, DB = 0, 1, 2
    near_own(T, 0)
    w_join(0)
    w_start(0)
    near_own(T, 1)
    w_join(1)
    w_start(1)
    w_near(0)
    w_pass(0, 0)
    act_four(T, 0)
    w_far(0)
    w_start(2)
    act_four(T, 1)
    near_own(C, 0)
    near_own(C, 1)
    w_near(1)
    w_pass(0, 1)
    w_pass(0, 2)
    w_pass(1, 0)
    w_pass(0, 3)
    w_far(1)
    w_near(2)
    w_pass(1, 1)
    w_pass(1, 2)
    w_end(0)
    w_pass(2, 0)
    w_far(2)
    w_pass(1, 3)
    act_four(C, 0)
    w_end(1)
    near_end(T, 0)
    near_end(T, 1)
    forward()
    term(M,4)
    sum_eight(M, 0)
    sum_eight(M, 1)
    sum_eight(M, 2)
    sum_eight(M, 3)
    term(M,2)
    near_two(M, 0)
    near_two(M, 1)
    near_two(M, 2)
    near_two(M, 3)
    w_pass(2, 1)
    act_four(C, 1)
    w_pass(2, 2)
    w_pass(2, 3)
    w_end(2)
    term(M,3)
    near_four(M, 0)
    near_four(M, 1)
    term(M,1)
    near_one(M, 0)
    near_one(M, 1)
    near_four(M, 2)
    near_four(M, 3)
    near_one(M, 2)
    near_one(M, 3)
    term(M,0)
    near_end(C, 0)
    near_end(C, 1)
    backward()
    term(G,4)
    sum_eight(G, 0)
    sum_eight(G, 1)
    sum_eight(G, 2)
    sum_eight(G, 3)
    term(G,2)
    near_two(G, 0)
    near_two(G, 1)
    term(G,3)
    near_four(G, 0)
    near_four(G, 1)
    near_two(G, 2)
    near_two(G, 3)
    near_four(G, 2)
    near_four(G, 3)
    term(G,1)
    near_one(G, 0)
    near_one(G, 1)
    near_one(G, 2)
    near_one(G, 3)
    term(G,0)
    near_sum(M, 0)
    near_sum(M, 1)
    near_sum(M, 2)
    near_sum(M, 3)
    near_sum(G, 0)
    near_sum(G, 1)
    near_sum(G, 2)
    near_sum(G, 3)
    for o in range(2):
        sends.arrive(outs[o].at[:, theirs], out_slot[o], sibling)
    for copy in last:
        copy.wait()
    for n in range(2):
        sends.left(alls[n].at[0, own_rows, :], swap_act_group[n], sibling)
        sends.left(stage.at[n, 1], swap_w_group[n], sibling)
        sends.left(alls[n].at[0:4], act_group[n], sibling)
        sends.left(sendbuf.at[n, 0:4], sum_group[n], sibling)
        sends.left(sendbuf.at[n, 0, sib_rows, :], out_group[n], sibling)
    for n, (array, first, end) in enumerate(parts):
        sends.left(gathered[array].at[first:end, 0:240, :], w_group[n], sibling)


def on_device(tokens, cotangent, up_weight, down_weight):
    any_spec = pl.BlockSpec(memory_space=pl.ANY)
    hbm_spec = pl.BlockSpec(memory_space=pltpu.HBM)
    bf, f32 = jnp.bfloat16, jnp.float32
    both = pl.pallas_call(
        kernel,
        out_shape=jax.ShapeDtypeStruct((2,) + tokens.shape, bf),
        in_specs=[hbm_spec] * 4,
        out_specs=any_spec,
        scratch_shapes=[
            pltpu.VMEM((TERMS, 2 * TOK, BLK), bf),
            pltpu.VMEM((TERMS, 2 * TOK, BLK), bf),
            pltpu.VMEM((TERMS, BLK, HB), bf),
            pltpu.VMEM((TERMS, BLK, HB), bf),
            pltpu.VMEM((2, 2, TERMS, 8, HB), bf),
            pltpu.VMEM((2, 2, 2 * TOK, BLK), f32),
            pltpu.VMEM((2, TERMS, 2 * TOK, BLK), bf),
            pltpu.VMEM((2, 4, 2 * TOK, BLK), bf),
            pltpu.VMEM((2 * TOK, HB), bf),
            pltpu.VMEM((2 * TOK, HB), f32),
            pltpu.VMEM((2 * TOK, HB), bf),
            pltpu.SemaphoreType.DMA((8,)),
            pltpu.SemaphoreType.DMA((SEND_SEMS,)),
            pltpu.SemaphoreType.DMA((RECV_SEMS,)),
        ],
        compiler_params=pltpu.CompilerParams(
            collective_id=0, has_side_effects=True, vmem_limit_bytes=48 * 1024 * 1024),
    )(*[pltpu.with_memory_space_constraint(v, pltpu.HBM) for v in (tokens, cotangent, up_weight, down_weight)])
    return both[0], both[1]


def solution(mesh):
    act, weight = P("dp", "mp"), P(None, "dp", "mp")
    return jax.shard_map(
        on_device, mesh=mesh, in_specs=(act, act, weight, weight), out_specs=(act, act), check_vma=False)
```

```python
import math

import jax
import jax.numpy as jnp
from jax import lax
from jax.experimental import pallas as pl
from jax.experimental.pallas import tpu as pltpu
from jax.sharding import PartitionSpec as P

BLK = 256
TERMS = 5
HB = 1024
TOK = 128
SIDE = 4
MESH = pl.DeviceIdType.MESH
ROOT = math.sqrt(2.0 / math.pi)
CUBE = 0.044715
SEND_SEMS, RECV_SEMS = 13, 51


def xor_step(bit, amount):
    return amount - 2 * amount * bit


class Sends:
    def __init__(self, send_sem, recv_sem):
        self.send_sem, self.recv_sem = send_sem, recv_sem
        self.groups, self.received = 0, 0

    def group(self):
        self.groups += 1
        return self.groups - 1

    def slot(self):
        self.received += 1
        return self.received - 1

    def start(self, src, dst, group, slot, device):
        pltpu.make_async_remote_copy(
            src_ref=src, dst_ref=dst, send_sem=self.send_sem.at[group],
            recv_sem=self.recv_sem.at[slot], device_id=device, device_id_type=MESH,
        ).start()

    def arrive(self, dst, slot, device):
        pltpu.make_async_remote_copy(
            src_ref=dst, dst_ref=dst, send_sem=self.send_sem.at[0],
            recv_sem=self.recv_sem.at[slot], device_id=device, device_id_type=MESH,
        ).wait_recv()

    def left(self, src, group, device):
        pltpu.make_async_remote_copy(
            src_ref=src, dst_ref=src, send_sem=self.send_sem.at[group],
            recv_sem=self.recv_sem.at[0], device_id=device, device_id_type=MESH,
        ).wait_send()


def kernel(tok, cot, up, down, both,
           x_all, c_all, wu, wd, stage, terms, sendbuf, landed, hidden, slope, gpre,
           local_sem, send_sem, recv_sem):
    dp = lax.axis_index("dp")
    z = lax.axis_index("mp")
    core = lax.rem(dp, 2)
    chip = lax.div(dp, 2)
    px, py = lax.rem(chip, SIDE), lax.div(chip, SIDE)
    a = px * (1 - core) + py * core
    b = py * (1 - core) + px * core

    def chip_at(a_pos, b_pos):
        return a_pos * (1 + 3 * core) + b_pos * (4 - 3 * core)

    def ring(pos, step):
        return lax.rem(pos + step + SIDE, SIDE)

    def plane(a_pos, b_pos):
        return (chip_at(a_pos, b_pos) * 2 + core, z)

    b0 = lax.rem(z, 2)
    b1 = lax.rem(lax.div(z, 2), 2)
    b2 = lax.rem(lax.div(z, 4), 2)
    b3 = lax.rem(lax.div(z, 8), 2)
    d1, d2, d4, d8 = xor_step(b0, 1), xor_step(b1, 2), xor_step(b2, 4), xor_step(b3, 8)

    def along(step):
        return (dp, z + step)

    sibling = (dp + 1 - 2 * core, z)
    sends = Sends(send_sem, recv_sem)

    mine = pl.ds(pl.multiple_of(core * BLK, BLK), BLK)
    theirs = pl.ds(pl.multiple_of((1 - core) * BLK, BLK), BLK)
    own_rows = pl.ds(pl.multiple_of(core * TOK, TOK), TOK)
    sib_rows = pl.ds(pl.multiple_of((1 - core) * TOK, TOK), TOK)
    cuts = (1, 1, 2, 2)

    def pieces(base, count):
        step = TOK // count
        return [pl.ds(pl.multiple_of(base * TOK + i * step, step), step) for i in range(count)]

    own_units = pl.ds(pl.multiple_of(core * HB, HB), HB)
    sib_units = pl.ds(pl.multiple_of((1 - core) * HB, HB), HB)
    acts, alls = (tok, cot), (x_all, c_all)
    weights, gathered = (up, down), (wu, wd)

    barrier = pltpu.get_barrier_semaphore()
    a_up, a_down, b_up, b_down = (
        plane(ring(a, 1), b), plane(ring(a, -1), b), plane(a, ring(b, 1)), plane(a, ring(b, -1)))
    greet = [along(s) for s in (d4 + d8, d4, d2, d1)]
    greet += [a_up, a_down, b_up, b_down, sibling]
    for device in greet:
        pl.semaphore_signal(barrier, inc=1, device_id=device, device_id_type=MESH)
    local = []
    for n in range(2):
        local.append(pltpu.make_async_copy(acts[n].at[:, mine], alls[n].at[0, own_rows, :], local_sem.at[n]))
        local.append(pltpu.make_async_copy(weights[n].at[:, :, own_units], stage.at[n, 0], local_sem.at[2 + n]))
    for copy in local:
        copy.start()

    pl.semaphore_wait(barrier, len(greet))

    swap_act = [sends.slot() for _ in range(2)]
    swap_w = [sends.slot() for _ in range(2)]
    swap_act_group = [sends.group() for _ in range(2)]
    swap_w_group = [sends.group() for _ in range(2)]
    for n in range(2):
        sends.start(acts[n].at[:, theirs], alls[n].at[0, own_rows, :], swap_act_group[n], swap_act[n], sibling)
        sends.start(weights[n].at[:, :, sib_units], stage.at[n, 1], swap_w_group[n], swap_w[n], sibling)

    act_rows = [pieces(core, cuts[n]) + pieces(1 - core, cuts[n]) for n in range(2)]
    near_slot = [[sends.slot() for _ in rows] for rows in act_rows]
    four_slot = [[sends.slot() for _ in rows] for rows in act_rows]
    act_group = [sends.group() for _ in range(2)]
    act_place = (0, 1, 2, 4, 3)

    def act_send(n, ch, src, dst, slot, device):
        rows = act_rows[n][ch]
        sends.start(alls[n].at[src, rows, :], alls[n].at[dst, rows, :], act_group[n], slot[n][ch], device)

    def act_four(n, ch):
        sends.arrive(alls[n].at[4, act_rows[n][ch], :], four_slot[n][ch], sibling)
        act_send(n, ch, 4, 3, near_slot, along(d4 + d8))

    def near_own(n, ch):
        if ch == 0:
            local[2 * n].wait()
        elif ch == cuts[n]:
            sends.arrive(alls[n].at[0, sib_rows, :], swap_act[n], sibling)
        act_send(n, ch, 0, 4, four_slot, along(d4))
        act_send(n, ch, 0, 2, near_slot, along(d2))
        act_send(n, ch, 0, 1, near_slot, along(d1))

    def near_end(n, ch):
        sends.arrive(alls[n].at[1:4, act_rows[n][ch], :], near_slot[n][ch], sibling)

    parts = ((0, 0, 5), (1, 2, 5), (1, 0, 2))
    w_slot = [[sends.slot() for _ in range(7)] for _ in parts]
    w_group = [sends.group() for _ in parts]
    ks = (a, ring(a, -1), ring(a, 1), ring(a, 2))
    lo, hi, whole = pl.ds(0, HB // 2), pl.ds(HB // 2, HB // 2), pl.ds(0, HB)

    def piece(n, a_pos, b_pos, cols):
        rows = pl.ds(pl.multiple_of(chip_at(a_pos, b_pos) * 16, 16), 16)
        array, first, end = parts[n]
        return gathered[array].at[first:end, rows, cols]

    def w_send(n, a_pos, b_pos, cols, slot, device):
        ref = piece(n, a_pos, b_pos, cols)
        sends.start(ref, ref, w_group[n], w_slot[n][slot], device)

    def w_wait(n, a_pos, b_pos, slot):
        sends.arrive(piece(n, a_pos, b_pos, whole), w_slot[n][slot], sibling)

    def w_across(n, k):
        w_send(n, ks[k], b, whole, 3 + k, b_up)
        w_send(n, ks[k], b, whole, 3 + k, b_down)

    def w_join(array):
        local[2 * array + 1].wait()
        sends.arrive(stage.at[array, 1], swap_w[array], sibling)
        first = stage[array, 0].astype(jnp.float32)
        second = stage[array, 1].astype(jnp.float32)
        rows = pl.ds(pl.multiple_of(chip * 16, 16), 16)

        @pl.when(core == 0)
        def _():
            gathered[array][:, rows, :] = jnp.concatenate([first, second], axis=1).astype(jnp.bfloat16)

        @pl.when(core == 1)
        def _():
            gathered[array][:, rows, :] = jnp.concatenate([second, first], axis=1).astype(jnp.bfloat16)

    def w_start(n):
        w_send(n, a, b, whole, 0, a_up)
        w_send(n, a, b, whole, 0, a_down)
        w_across(n, 0)

    def w_near(n):
        array, first, end = parts[n]
        sends.arrive(gathered[array].at[first:end, 0:32, :], w_slot[n][0], sibling)
        w_send(n, ks[1], b, lo, 2, a_up)
        w_send(n, ks[2], b, hi, 2, a_down)
        w_across(n, 1)
        w_across(n, 2)

    def w_far(n):
        w_wait(n, ks[3], b, 2)
        w_across(n, 3)

    def w_pass(n, k):
        array, first, end = parts[n]
        sends.arrive(gathered[array].at[first:end, 0:32, :], w_slot[n][3 + k], sibling)
        w_send(n, ks[k], ring(b, -1), lo, 1, b_up)
        w_send(n, ks[k], ring(b, 1), hi, 1, b_down)

    def w_end(n):
        array, first, end = parts[n]
        sends.arrive(gathered[array].at[first:end, 0:64, :], w_slot[n][1], sibling)

    TILE = 256

    def product(all_ref, w_ref, cols):
        total = None
        for s in range(TERMS):
            part = jnp.dot(all_ref[act_place[s]], w_ref[s, :, cols], preferred_element_type=jnp.float32)
            total = part if total is None else total + part
        return total

    def forward():
        def body(tile, carry):
            cols = pl.ds(pl.multiple_of(tile * TILE, TILE), TILE)
            pre = product(x_all, wu, cols)
            th = jnp.tanh(ROOT * (pre + CUBE * pre * pre * pre))
            hidden[:, cols] = (0.5 * pre * (1.0 + th)).astype(jnp.bfloat16)
            inner = ROOT * (1.0 + 3.0 * CUBE * pre * pre)
            slope[:, cols] = 0.5 * (1.0 + th) + 0.5 * pre * (1.0 - th * th) * inner
            return carry
        lax.fori_loop(0, HB // TILE, body, 0)

    def backward():
        def body(tile, carry):
            cols = pl.ds(pl.multiple_of(tile * TILE, TILE), TILE)
            gpre[:, cols] = (product(c_all, wd, cols) * slope[:, cols]).astype(jnp.bfloat16)
            return carry
        lax.fori_loop(0, HB // TILE, body, 0)

    def term(o, s):
        act_ref, w_ref = ((hidden, wd), (gpre, wu))[o]
        total = lax.dot_general(
            act_ref[...], w_ref[s], (((1,), (1,)), ((), ())), preferred_element_type=jnp.float32)
        if s in (0, 3):
            terms[o, s // 3] = total
        else:
            sendbuf[o, s] = total.astype(jnp.bfloat16)

    sum_rows = [pieces(1 - core, cuts[2 + o]) + pieces(core, cuts[2 + o]) for o in range(2)]
    first_slot = [[sends.slot() for _ in rows] for rows in sum_rows]
    last_slot = [[sends.slot() for _ in rows] for rows in sum_rows]
    sum_group = [sends.group() for _ in range(2)]
    out_slot = [sends.slot() for _ in range(2)]
    out_group = [sends.group() for _ in range(2)]
    outs = (both.at[0], both.at[1])
    last = []

    def sum_send(o, ch, s, place, slot, device):
        rows = sum_rows[o][ch]
        sends.start(sendbuf.at[o, s, rows, :], landed.at[o, place, rows, :], sum_group[o], slot[o][ch], device)

    def sum_eight(o, ch):
        sum_send(o, ch, 4, 3, first_slot, along(d4 + d8))

    def near_two(o, ch):
        sum_send(o, ch, 2, 1, last_slot, along(d2))

    def near_one(o, ch):
        sum_send(o, ch, 1, 0, last_slot, along(d1))

    def near_four(o, ch):
        rows = sum_rows[o][ch]
        sends.arrive(landed.at[o, 3, rows, :], first_slot[o][ch], sibling)
        total = terms[o, 1, rows, :] + landed[o, 3, rows, :].astype(jnp.float32)
        sendbuf[o, 3, rows, :] = total.astype(jnp.bfloat16)
        sum_send(o, ch, 3, 2, last_slot, along(d4))

    def near_sum(o, ch):
        rows = sum_rows[o][ch]
        sends.arrive(landed.at[o, 0:3, rows, :], last_slot[o][ch], sibling)
        total = terms[o, 0, rows, :]
        for place in range(3):
            total = total + landed[o, place, rows, :].astype(jnp.float32)
        sendbuf[o, 0, rows, :] = total.astype(jnp.bfloat16)
        here = pl.ds(ch % cuts[2 + o] * (TOK // cuts[2 + o]), TOK // cuts[2 + o])
        place = outs[o].at[here, mine]
        if ch < cuts[2 + o]:
            sends.start(sendbuf.at[o, 0, rows, :], place, out_group[o], out_slot[o], sibling)
        else:
            copy = pltpu.make_async_copy(sendbuf.at[o, 0, rows, :], place, local_sem.at[4 + 2 * o + ch % cuts[2 + o]])
            copy.start()
            last.append(copy)

    T, C, M, G = 0, 1, 0, 1
    UP, DA, DB = 0, 1, 2
    near_own(T, 0)
    w_join(0)
    w_start(0)
    near_own(T, 1)
    w_join(1)
    w_start(1)
    w_near(0)
    w_pass(0, 0)
    act_four(T, 0)
    w_far(0)
    w_start(2)
    act_four(T, 1)
    near_own(C, 0)
    near_own(C, 1)
    w_near(1)
    w_pass(0, 1)
    w_pass(0, 2)
    w_pass(1, 0)
    w_pass(0, 3)
    w_far(1)
    w_near(2)
    w_pass(1, 1)
    w_pass(1, 2)
    w_end(0)
    w_pass(2, 0)
    w_far(2)
    w_pass(1, 3)
    act_four(C, 0)
    w_end(1)
    near_end(T, 0)
    near_end(T, 1)
    forward()
    term(M,4)
    sum_eight(M, 0)
    sum_eight(M, 1)
    sum_eight(M, 2)
    sum_eight(M, 3)
    term(M,2)
    near_two(M, 0)
    near_two(M, 1)
    near_two(M, 2)
    near_two(M, 3)
    w_pass(2, 1)
    act_four(C, 1)
    w_pass(2, 2)
    w_pass(2, 3)
    w_end(2)
    term(M,3)
    near_four(M, 0)
    near_four(M, 1)
    term(M,1)
    near_one(M, 0)
    near_one(M, 1)
    near_four(M, 2)
    near_four(M, 3)
    near_one(M, 2)
    near_one(M, 3)
    term(M,0)
    near_end(C, 0)
    near_end(C, 1)
    backward()
    term(G,4)
    sum_eight(G, 0)
    sum_eight(G, 1)
    sum_eight(G, 2)
    sum_eight(G, 3)
    term(G,2)
    near_two(G, 0)
    near_two(G, 1)
    term(G,3)
    near_four(G, 0)
    near_four(G, 1)
    near_two(G, 2)
    near_two(G, 3)
    near_four(G, 2)
    near_four(G, 3)
    term(G,1)
    near_one(G, 0)
    near_one(G, 1)
    near_one(G, 2)
    near_one(G, 3)
    term(G,0)
    near_sum(M, 0)
    near_sum(M, 1)
    near_sum(M, 2)
    near_sum(M, 3)
    near_sum(G, 0)
    near_sum(G, 1)
    near_sum(G, 2)
    near_sum(G, 3)
    for o in range(2):
        sends.arrive(outs[o].at[:, theirs], out_slot[o], sibling)
    for copy in last:
        copy.wait()
    for n in range(2):
        sends.left(alls[n].at[0, own_rows, :], swap_act_group[n], sibling)
        sends.left(stage.at[n, 1], swap_w_group[n], sibling)
        sends.left(alls[n].at[0:4], act_group[n], sibling)
        sends.left(sendbuf.at[n, 0:4], sum_group[n], sibling)
        sends.left(sendbuf.at[n, 0, sib_rows, :], out_group[n], sibling)
    for n, (array, first, end) in enumerate(parts):
        sends.left(gathered[array].at[first:end, 0:240, :], w_group[n], sibling)


def on_device(tokens, cotangent, up_weight, down_weight):
    any_spec = pl.BlockSpec(memory_space=pl.ANY)
    hbm_spec = pl.BlockSpec(memory_space=pltpu.HBM)
    bf, f32 = jnp.bfloat16, jnp.float32
    both = pl.pallas_call(
        kernel,
        out_shape=jax.ShapeDtypeStruct((2,) + tokens.shape, bf),
        in_specs=[hbm_spec] * 4,
        out_specs=any_spec,
        scratch_shapes=[
            pltpu.VMEM((TERMS, 2 * TOK, BLK), bf),
            pltpu.VMEM((TERMS, 2 * TOK, BLK), bf),
            pltpu.VMEM((TERMS, BLK, HB), bf),
            pltpu.VMEM((TERMS, BLK, HB), bf),
            pltpu.VMEM((2, 2, TERMS, 8, HB), bf),
            pltpu.VMEM((2, 2, 2 * TOK, BLK), f32),
            pltpu.VMEM((2, TERMS, 2 * TOK, BLK), bf),
            pltpu.VMEM((2, 4, 2 * TOK, BLK), bf),
            pltpu.VMEM((2 * TOK, HB), bf),
            pltpu.VMEM((2 * TOK, HB), f32),
            pltpu.VMEM((2 * TOK, HB), bf),
            pltpu.SemaphoreType.DMA((8,)),
            pltpu.SemaphoreType.DMA((SEND_SEMS,)),
            pltpu.SemaphoreType.DMA((RECV_SEMS,)),
        ],
        compiler_params=pltpu.CompilerParams(
            collective_id=0, has_side_effects=True, vmem_limit_bytes=48 * 1024 * 1024),
    )(*[pltpu.with_memory_space_constraint(v, pltpu.HBM) for v in (tokens, cotangent, up_weight, down_weight)])
    return both[0], both[1]


def solution(mesh):
    act, weight = P("dp", "mp"), P(None, "dp", "mp")
    return jax.shard_map(
        on_device, mesh=mesh, in_specs=(act, act, weight, weight), out_specs=(act, act), check_vma=False)
```
